128 devices in a mesh: src: 8 (over y, core), rcv: 16 (over x, z).
Axes of the slice: x: 4, y: 4, z: 4, core: 2. Of those that a mesh axis runs over, the one named last changes fastest.
Arguments:
- data: bfloat16 [2, 8192, 8192], P(None, ('src', 'rcv')), may hold values from -0.8984375 to 0.8984375
- fill_mask: int32 [8192, 8192], P(('src', 'rcv')), may hold values 0 or 1
- obliquity: float32 [8192], replicated, may hold values from 0.25 to 4
- aperture: int32 [16, 16, 8], P('src'), may hold values from 0 to 15, as said below
- lengths: int32 [16, 16], P('src', 'rcv'), may hold values from 1 to 8, as said below
Outputs:
- predicted: float32 [2, 8192, 8192], P(None, 'src', 'rcv')
The draws below stay inside these ranges and needn't reach their ends.
Inputs may be any that keep to these rules, and one draw needn't show every extreme that they name: `aperture`: every entry is a tile index; the 8 entries of one output tile are distinct; only the first lengths entries of a list are used. `lengths`: some output tile uses all 8 entries of its list.
All inputs are finite; a program needn't handle non-finite values. No bound on the sum of `fill_mask` on one device may be relied on, other than what follows from the above.
Results may differ from the reference program's by a relative error of at most 0.0028.
Values may be sent and summed in bfloat16 or wider, within the bound.
A program may use at most 128 MiB of HBM per device.

```python
import math
import jax
import jax.numpy as jnp
from jax import lax

TILE_SIZE = 512
MAX_SLOTS = 8
TILE_COUNT = 16
STATIONS = 8192


def draw_aperture(key, part):
    local_key = jax.random.fold_in(key, 11)
    scores = jax.random.randint(local_key, (TILE_COUNT, TILE_COUNT, TILE_COUNT), 0, 2 ** 20, dtype=jnp.int32)
    scores = scores * TILE_COUNT + jnp.arange(TILE_COUNT, dtype=jnp.int32)
    ordering = jnp.argsort(scores, axis=-1, stable=True)
    return ordering[:, :, :MAX_SLOTS].astype(jnp.int32)


def draw_lengths(key, part):
    local_key = jax.random.fold_in(key, 23)
    first_key, second_key, third_key = jax.random.split(local_key, 3)
    first_draw = jax.random.randint(first_key, (TILE_COUNT, TILE_COUNT), 0, MAX_SLOTS, dtype=jnp.int32)
    second_draw = jax.random.randint(second_key, (TILE_COUNT, TILE_COUNT), 0, MAX_SLOTS, dtype=jnp.int32)
    counts = MAX_SLOTS - first_draw * second_draw // (MAX_SLOTS - 1)
    forced = jax.random.randint(third_key, (), 0, TILE_COUNT * TILE_COUNT, dtype=jnp.int32)
    counts = counts.reshape(-1).at[forced].set(MAX_SLOTS)
    return counts.reshape(TILE_COUNT, TILE_COUNT).astype(jnp.int32)


def plant(array, own_key, smallest, largest):
    dims = array.shape
    index_at = [jax.random.randint(jax.random.fold_in(own_key, axis), (), 0, dims[axis]) for axis in range(len(dims))]
    array = array.at[tuple(index_at)].set(smallest)
    longest = dims.index(max(dims))
    index_at[longest] = (index_at[longest] + 1) % dims[longest]
    return array.at[tuple(index_at)].set(largest)


def level_of(key, extent, pieces, least, top_value):
    gain, own = 1.0, jax.random.fold_in(key, 6)
    for position, shards_of in pieces:
        draws = jnp.exp(jax.random.uniform(jax.random.fold_in(own, position), (shards_of,), jnp.float32, least / len(pieces), top_value / len(pieces)))
        gain = gain * jnp.repeat(draws, extent[position] // shards_of).reshape([-1 if axis == position else 1 for axis in range(len(extent))])
    return gain


def gaussian(own_key, dims, deviation, most, pieces=(), kind=jnp.bfloat16):
    factor_of = level_of(own_key, dims, pieces, -0.22, 0.18) if pieces else 1.0
    result = jax.random.normal(own_key, dims, jnp.float32) * deviation * factor_of
    return jnp.minimum(jnp.maximum(result, -most), most).astype(kind)


def setup_inputs(seed: int = 0) -> dict:
    keys = jax.random.split(jax.random.key(seed), 6)
    return {
        "data": gaussian(keys[0], (2, STATIONS, STATIONS), 0.15, 0.8984375, ((1, 128),)),
        "fill_mask": plant((jax.random.randint(keys[1], (STATIONS, STATIONS), 0, 3) < 2).astype(jnp.int32), jax.random.fold_in(keys[1], 1), 0, 1),
        "obliquity": jnp.clip(jnp.exp(jax.random.uniform(keys[2], (STATIONS,), jnp.float32, math.log(0.25), math.log(4.0))), 0.25, 4.0),
        "aperture": draw_aperture(jax.random.fold_in(keys[5], 71), 0),
        "lengths": draw_lengths(jax.random.fold_in(keys[5], 71), 0),
    }


def complex_product(left_pair, right_pair):
    left_wide = jnp.concatenate([left_pair[0], left_pair[1]], axis=1)
    upper = jnp.concatenate([right_pair[0], right_pair[1]], axis=1)
    lower = jnp.concatenate([-right_pair[1], right_pair[0]], axis=1)
    right_wide = jnp.concatenate([upper, lower], axis=0)
    return jnp.dot(left_wide, right_wide, preferred_element_type=jnp.float32)


def reference(data, fill_mask, obliquity, aperture, lengths):
    transposed = jnp.swapaxes(data, 1, 2)
    filled = jnp.where(fill_mask[None] == 1, data, transposed)
    weighted = (filled.astype(jnp.float32) * obliquity[None, :, None]).astype(jnp.bfloat16)

    def predict_tile(flat_index):
        tile_row = (flat_index // TILE_COUNT).astype(jnp.int32)
        tile_col = (flat_index % TILE_COUNT).astype(jnp.int32)

        def add_slot(slot_index, summed):
            inner_tile = aperture[tile_row, tile_col, slot_index].astype(jnp.int32)
            left_pair = lax.dynamic_slice(filled, (jnp.int32(0), tile_row * TILE_SIZE, inner_tile * TILE_SIZE), (2, TILE_SIZE, TILE_SIZE))
            right_pair = lax.dynamic_slice(weighted, (jnp.int32(0), inner_tile * TILE_SIZE, tile_col * TILE_SIZE), (2, TILE_SIZE, TILE_SIZE))
            return summed + complex_product(left_pair, right_pair)

        initial = jnp.zeros((TILE_SIZE, 2 * TILE_SIZE), jnp.float32)
        return -lax.fori_loop(0, lengths[tile_row, tile_col], add_slot, initial)

    results = lax.map(predict_tile, jnp.arange(TILE_COUNT * TILE_COUNT, dtype=jnp.int32))
    results = results.reshape(TILE_COUNT, TILE_COUNT, TILE_SIZE, 2, TILE_SIZE)
    results = jnp.transpose(results, (3, 0, 2, 1, 4))
    return results.reshape(2, STATIONS, STATIONS)
```

```python
import jax
import jax.numpy as jnp
from jax import lax
from jax.experimental import pallas as pl
from jax.experimental.pallas import tpu as pltpu
from jax.sharding import PartitionSpec as P

TILE = 512
SLOTS = 8
TILES = 16
ROWS = 64
DEVICES = 128
MESH = pl.DeviceIdType.MESH
F32 = jnp.float32
BF16 = jnp.bfloat16

OFFSET = (0, 3, 1, 2)


def kernel(
    data, mask, gain, lens, aperture,
    out,
    xt, recv, wb, a_out, a0, a1, a2, a3, b0, b1, b2, b3, c_out, c_in, acc, lens_all, lens_s,
    p1_send, p1_recv, l_send, l_recv, l_copy, a2_send, a2_recv, b2_send, b2_recv,
    a3_send, a3_recv, b3_send, b3_recv, s_send, s_recv, c_send, c_recv,
):
    src, rcv = lax.axis_index("src"), lax.axis_index("rcv")
    y, core = src // 2, src % 2
    x, z = rcv // 4, rcv % 4
    me = src * 16 + rcv
    a_bufs = (a0, a1, a2, a3)
    b_bufs = (b0, b1, b2, b3)

    def device(yy, cc, xx, zz):
        return (yy * 2 + cc, xx * 4 + zz)

    def remote(source, target, send, got, to):
        return pltpu.make_async_remote_copy(
            src_ref=source, dst_ref=target, send_sem=send, recv_sem=got,
            device_id=to, device_id_type=MESH,
        )

    lens_all[z] = lens[...]
    length_copies = []
    for k in range(1, 4):
        copy = remote(lens, lens_all.at[z], l_send.at[k - 1], l_recv.at[k - 1],
                      device(y, core, x, (z + k) % 4))
        copy.start()
        length_copies.append(copy)

    def turn(q):
        block = data[:, :, pl.ds(pl.multiple_of(q * 128, 128), 128)].reshape(128, 128)
        xt[pl.ds(q * 2, 2)] = block.T.reshape(2, ROWS, 128)

    def block_copy(target):
        return remote(xt.at[target], recv.at[me], p1_send, p1_recv.at[me // 8],
                      (target // 16, target % 16))

    turn(me // 2)
    own = pltpu.make_async_copy(xt.at[me], recv.at[me], p1_recv.at[me // 8])
    own.start()
    block_copy(me + 1 - 2 * (me % 2)).start()

    @pl.loop(1, 64)
    def _(k):
        q = (me // 2 + k) % 64
        turn(q)
        block_copy(q * 2).start()
        block_copy(q * 2 + 1).start()

    for buf in a_bufs:
        buf[TILES] = jnp.zeros((4, ROWS, 256), BF16)

    lane = lax.broadcasted_iota(jnp.int32, (ROWS, 128), 1)
    low = lane < ROWS
    row = lax.broadcasted_iota(jnp.int32, (ROWS, 128), 0)
    gain_row = jnp.broadcast_to(gain[pl.ds(me // 2, 1), :], (ROWS, 128))
    gains = jnp.sum(
        jnp.where(lane == row + (me % 2) * ROWS, gain_row, 0.0), axis=1, keepdims=True
    )

    def join(first, second):
        return jnp.where(low, first, second)

    def swap(value):
        return pltpu.roll(value, ROWS, 1)

    tile_me = src * 2 + x // 2

    def right_copy(tile):
        to_y = (tile % 4 - z + 4) % 4
        return remote(wb.at[tile], b0.at[tile_me, :, x % 2], b2_send.at[tile], b2_recv.at[y],
                      device(to_y, core, tile // 4, z))

    def is_mine(tile):
        return jnp.logical_and((tile % 4 - z + 4) % 4 == y, tile // 4 == x)

    def right_own(tile):
        return pltpu.make_async_copy(wb.at[tile], b0.at[tile_me, :, x % 2], b2_recv.at[y])

    @pl.loop(0, TILES)
    def _(tile):
        group = recv.at[pl.ds(tile * 8, 8)]
        pltpu.make_async_copy(group, group, p1_recv.at[tile]).wait()
        filled = []
        for q in range(4):
            columns = pl.ds(pl.multiple_of(tile * 512 + q * 128, 128), 128)
            first = recv[tile * 8 + 2 * q].astype(F32)
            second = recv[tile * 8 + 2 * q + 1].astype(F32)
            turned = (join(first, swap(second)), join(swap(first), second))
            keep = mask[:, columns] == 1
            pair = []
            for part in range(2):
                value = jnp.where(keep, data[part, :, columns].astype(F32), turned[part])
                wb[tile, part, :, q * 128:(q + 1) * 128] = (value * gains).astype(BF16)
                pair.append(value)
            filled.append(pair)
        for part in range(2):
            lanes = slice((1 - part) * 128, (2 - part) * 128)
            for half in range(2):
                first, second = filled[half][part], filled[2 + half][part]
                a_out[2 * half, tile, :, lanes] = (-join(first, swap(second))).astype(BF16)
                a_out[2 * half + 1, tile, :, lanes] = (-join(swap(first), second)).astype(BF16)

        @pl.when(is_mine(tile))
        def _():
            right_own(tile).start()

        @pl.when(jnp.logical_not(is_mine(tile)))
        def _():
            right_copy(tile).start()

    pltpu.make_async_copy(a_out.at[z], a0.at[pl.ds(0, TILES), z], a2_recv.at[z]).start()
    left_copies = []
    for k in range(1, 4):
        to = (z + k) % 4
        copy = remote(a_out.at[to], a0.at[pl.ds(0, TILES), z], a2_send.at[k - 1], a2_recv.at[z],
                      device(y, core, x, to))
        copy.start()
        left_copies.append(copy)

    def a_copy(part, from_slot, to_slot, step, index):
        return remote(
            a_bufs[from_slot].at[pl.ds(0, TILES), part],
            a_bufs[to_slot].at[pl.ds(0, TILES), part],
            a3_send.at[index], a3_recv.at[to_slot - 1, part],
            device(y, core, (x + step) % 4, z),
        )

    def b_block(slot, part, which):
        return b_bufs[slot].at[pl.ds(part * 4 + which * 2, 2)]

    def b_copy(part, from_slot, to_slot, step, index):
        return remote(
            b_block(from_slot, part, core), b_block(to_slot, part, core),
            b3_send.at[index], b3_recv.at[to_slot - 1, part],
            device((y + step) % 4, core, x, z),
        )

    def sibling_copy(slot, part):
        return remote(
            b_block(slot, part, core), b_block(slot, part, core),
            s_send.at[slot, part], s_recv.at[slot, part], device(y, 1 - core, x, z),
        )

    def wait_on(ref, sem):
        pltpu.make_async_copy(ref, ref, sem).wait()

    sends = []

    def start(copy):
        copy.start()
        sends.append(copy)

    for part in range(4):
        wait_on(b_block(0, part, core), b2_recv.at[part])
        start(b_copy(part, 0, 1, 1, part))
        start(b_copy(part, 0, 2, 3, 4 + part))
        start(sibling_copy(0, part))
        wait_on(a0.at[pl.ds(0, TILES), part], a2_recv.at[part])
        start(a_copy(part, 0, 1, 1, part))
        start(a_copy(part, 0, 2, 3, 4 + part))

    for k in range(1, 4):
        length_copies[k - 1].wait_recv()
    pltpu.make_async_copy(lens_all, lens_s, l_copy).start()
    pltpu.make_async_copy(lens_all, lens_s, l_copy).wait()

    def unit(a_slot, b_slot):
        a_buf, b_buf = a_bufs[a_slot], b_bufs[b_slot]
        piece = (x + OFFSET[a_slot]) % 4
        column = (y + OFFSET[b_slot] + z) % 4
        used = lens_s[column, piece // 2, 0]

        def product(slot):
            inner = aperture[piece // 2, x * 4 + column, slot]
            left = a_buf[jnp.where(slot < used, inner, TILES)].reshape(256, 256)
            right = b_buf[inner].reshape(256, 512)
            upper = jnp.concatenate([left[:, 128:], -left[:, :128]], axis=1)
            wide = jnp.concatenate([upper, left], axis=0)
            return jnp.dot(wide, right, preferred_element_type=F32)

        acc[...] = product(0)

        @pl.loop(1, SLOTS)
        def _(slot):
            acc[...] += product(slot)

        mine = column == z

        @pl.when(mine)
        def _():
            out[:, pl.ds(pl.multiple_of(piece * 256, 256), 256), :] = acc[...].reshape(2, 256, TILE)

        @pl.when(jnp.logical_not(mine))
        def _():
            c_out[a_slot, b_slot] = acc[...].reshape(2, 256, TILE).astype(BF16)
            result_copy(a_slot, b_slot).start()

    def result_copy(a_slot, b_slot):
        piece = (x + OFFSET[a_slot]) % 4
        column = (y + OFFSET[b_slot] + z) % 4
        behind = (z - column + 4) % 4 - 1
        return remote(
            c_out.at[a_slot, b_slot], c_in.at[behind, piece],
            c_send.at[a_slot, b_slot], c_recv.at[behind, piece], device(y, core, x, column),
        )

    for part in range(4):
        sibling_copy(0, part).wait_recv()
    unit(0, 0)

    def wait_a(slot, part):
        wait_on(a_bufs[slot].at[pl.ds(0, TILES), part], a3_recv.at[slot - 1, part])

    def wait_b(slot, part):
        wait_on(b_block(slot, part, core), b3_recv.at[slot - 1, part])

    for part in range(4):
        for slot in (1, 2):
            forward = part // 2 == slot - 1
            step = 1 if slot == 1 else 3
            wait_b(slot, part)
            if forward:
                start(b_copy(part, slot, 3, step, 8 + part))
            start(sibling_copy(slot, part))
            wait_a(slot, part)
            if forward:
                start(a_copy(part, slot, 3, step, 8 + part))
    for slot in (1, 2):
        for part in range(4):
            sibling_copy(slot, part).wait_recv()
    for pair in ((1, 0), (0, 1), (1, 1), (2, 0), (0, 2), (2, 1), (1, 2), (2, 2)):
        unit(*pair)
    for part in range(4):
        wait_b(3, part)
        start(sibling_copy(3, part))
    for part in range(4):
        wait_a(3, part)
        sibling_copy(3, part).wait_recv()
    for pair in ((3, 0), (0, 3), (3, 1), (1, 3), (3, 2), (2, 3), (3, 3)):
        unit(*pair)

    for piece in range(4):
        for behind in range(3):
            wait_on(c_in.at[behind, piece], c_recv.at[behind, piece])

        @pl.loop(0, 8)
        def _(step):
            rows = pl.ds(pl.multiple_of(step * 32, 32), 32)
            target = pl.ds(pl.multiple_of(piece * 256 + step * 32, 32), 32)
            total = out[:, target, :]
            for behind in range(3):
                total += c_in[behind, piece, :, rows, :].astype(F32)
            out[:, target, :] = total

    sent = xt.at[pl.ds(0, DEVICES - 1)]
    pltpu.make_async_copy(sent, sent, p1_send).wait()
    for copy in length_copies + left_copies + sends:
        copy.wait_send()

    @pl.loop(0, TILES)
    def _(tile):
        @pl.when(jnp.logical_not(is_mine(tile)))
        def _():
            right_copy(tile).wait_send()

    for a_slot in range(4):
        for b_slot in range(4):
            @pl.when((y + OFFSET[b_slot]) % 4 != 0)
            def _():
                result_copy(a_slot, b_slot).wait_send()


def local(data, fill_mask, obliquity, aperture, lengths):
    vmem = pl.BlockSpec(memory_space=pltpu.VMEM)
    dma = pltpu.SemaphoreType.DMA
    lens = jnp.pad(jnp.broadcast_to(lengths, (2, 128)), ((0, 6), (0, 0)))
    return pl.pallas_call(
        kernel,
        out_shape=jax.ShapeDtypeStruct((2, 2 * TILE, TILE), F32),
        in_specs=[vmem, vmem, vmem, vmem, pl.BlockSpec(memory_space=pltpu.SMEM)],
        out_specs=vmem,
        scratch_shapes=[
            pltpu.VMEM((DEVICES, ROWS, 128), BF16),
            pltpu.VMEM((DEVICES, ROWS, 128), BF16),
            pltpu.VMEM((TILES, 2, ROWS, TILE), BF16),
            pltpu.VMEM((4, TILES, ROWS, 256), BF16),
        ]
        + [pltpu.VMEM((TILES + 1, 4, ROWS, 256), BF16)] * 4
        + [pltpu.VMEM((TILES, 2, 2, ROWS, TILE), BF16)] * 4
        + [
            pltpu.VMEM((4, 4, 2, 256, TILE), BF16),
            pltpu.VMEM((3, 4, 2, 256, TILE), BF16),
            pltpu.VMEM((TILE, TILE), F32),
            pltpu.VMEM((4, 8, 128), jnp.int32),
            pltpu.SMEM((4, 8, 128), jnp.int32),
            dma(()), dma((16,)), dma((3,)), dma((3,)), dma(()), dma((3,)), dma((4,)), dma((16,)), dma((4,)),
            dma((12,)), dma((3, 4)), dma((12,)), dma((3, 4)), dma((4, 4)), dma((4, 4)), dma((4, 4)), dma((3, 4)),
        ],
        compiler_params=pltpu.CompilerParams(
            has_side_effects=True, vmem_limit_bytes=63 * 1024 * 1024
        ),
        cost_estimate=pl.CostEstimate(
            flops=17_000_000_000, bytes_accessed=10_000_000, transcendentals=0
        ),
    )(data, fill_mask, obliquity.reshape(64, 128), lens, aperture)


def solution(mesh):
    placed = (
        P(None, ("src", "rcv"), None),
        P(("src", "rcv"), None),
        P(),
        P("src", None, None),
        P("src", "rcv"),
    )
    return jax.shard_map(
        local, mesh=mesh, in_specs=placed, out_specs=P(None, "src", "rcv"), check_vma=False
    )
```

```python
import jax
import jax.numpy as jnp
from jax import lax
from jax.experimental import pallas as pl
from jax.experimental.pallas import tpu as pltpu
from jax.sharding import PartitionSpec as P

TILE = 512
SLOTS = 8
TILES = 16
ROWS = 64
DEVICES = 128
MESH = pl.DeviceIdType.MESH
F32 = jnp.float32
BF16 = jnp.bfloat16


def kernel(
    data, mask, gain, lens, aperture,
    c_in,
    xt, recv, wb, a_out, a0, a1, a2, a3, b0, b1, b2, b3, c_out, lens_own, lens_all, lens_s, lists,
    p1_send, p1_recv, l_send, l_recv, l_copy, a2_send, a2_recv, b2_send, b2_recv,
    a3_send, a3_recv, b3_send, b3_recv, s_send, s_recv, c_send, c_recv,
):
    src, rcv = lax.axis_index("src"), lax.axis_index("rcv")
    y, core = src // 2, src % 2
    x, z = rcv // 4, rcv % 4
    me = src * 16 + rcv
    lefts = (a0, a1, a2, a3)
    rights = (b0, b1, b2, b3)

    def device(yy, cc, xx, zz):
        return (yy * 2 + cc, xx * 4 + zz)

    def remote(source, target, send, got, to):
        return pltpu.make_async_remote_copy(
            src_ref=source, dst_ref=target, send_sem=send, recv_sem=got,
            device_id=to, device_id_type=MESH,
        )

    def wait_on(ref, sem):
        pltpu.make_async_copy(ref, ref, sem).wait()

    list_copy = pltpu.make_async_copy(aperture, lists, l_copy.at[0])
    list_copy.start()

    eye = (
        lax.broadcasted_iota(jnp.int32, (256, 256), 0)
        == lax.broadcasted_iota(jnp.int32, (256, 256), 1)
    ).astype(F32).astype(BF16)

    def turn(q):
        block = data[:, :, pl.ds(pl.multiple_of(q * 256, 256), 256)].reshape(128, 256)
        turned = lax.dot_general(
            eye, block, (((1,), (1,)), ((), ())), preferred_element_type=F32
        )
        xt[pl.ds(q * 4, 4)] = turned.astype(BF16).reshape(4, ROWS, 128)

    def block_copy(target):
        return remote(xt.at[target], recv.at[me], p1_send, p1_recv.at[me // 8],
                      (target // 16, target % 16))

    turn(me // 4)
    pltpu.make_async_copy(xt.at[me], recv.at[me], p1_recv.at[me // 8]).start()
    for i in range(1, 4):
        block_copy(me // 4 * 4 + (me + i) % 4).start()

    @pl.loop(1, 32)
    def _(k):
        q = (me // 4 + k) % 32
        turn(q)
        for i in range(4):
            block_copy(q * 4 + (me + i) % 4).start()

    lens_own[0:1, :] = jnp.broadcast_to(lens[:, 0:1], (1, 128))
    lens_own[1:2, :] = jnp.broadcast_to(lens[:, 1:2], (1, 128))
    lens_own[2:8, :] = jnp.zeros((6, 128), jnp.int32)
    lens_all[z] = lens_own[...]
    length_copies = []
    for k in range(1, 4):
        copy = remote(lens_own, lens_all.at[z], l_send.at[k - 1], l_recv.at[k - 1],
                      device(y, core, x, (z + k) % 4))
        copy.start()
        length_copies.append(copy)

    for buf in lefts:
        for e in range(2):
            buf[e, TILES] = jnp.zeros((4, 32, 256), BF16)

    lane = lax.broadcasted_iota(jnp.int32, (ROWS, 128), 1)
    low = lane < ROWS
    row = lax.broadcasted_iota(jnp.int32, (ROWS, 128), 0)
    gain_row = jnp.broadcast_to(gain[pl.ds(me // 2, 1), :], (ROWS, 128))
    gains = jnp.sum(
        jnp.where(lane == row + (me % 2) * ROWS, gain_row, 0.0), axis=1, keepdims=True
    )

    def join(first, second):
        return jnp.where(low, first, second)

    def swap(value):
        return pltpu.roll(value, ROWS, 1)

    @pl.loop(0, TILES)
    def _(step):
        tile = (me // 8 - step - 1 + x % 2 + TILES) % TILES
        group = recv.at[pl.ds(tile * 8, 8)]
        wait_on(group, p1_recv.at[tile])
        filled = []
        for q in range(4):
            columns = pl.ds(pl.multiple_of(tile * 512 + q * 128, 128), 128)
            first = recv[tile * 8 + 2 * q].astype(F32)
            second = recv[tile * 8 + 2 * q + 1].astype(F32)
            turned = (join(first, swap(second)), join(swap(first), second))
            keep = mask[:, columns] == 1
            pair = []
            for part in range(2):
                value = jnp.where(keep, data[part, :, columns].astype(F32), turned[part])
                weighted = (value * gains).astype(BF16)
                wb[tile, q // 2, part, :, q % 2 * 128:(q % 2 + 1) * 128] = weighted
                pair.append(value)
            filled.append(pair)
        for part in range(2):
            lanes = slice((1 - part) * 128, (2 - part) * 128)
            for half in range(2):
                first, second = filled[half][part], filled[2 + half][part]
                for odd, value in ((0, join(first, swap(second))), (1, join(swap(first), second))):
                    value = (-value).astype(BF16)
                    a_out[2 * half + odd, 0, tile, :, lanes] = value[:32]
                    a_out[2 * half + odd, 1, tile, :, lanes] = value[32:]

        d = (z - tile % 4 + 4) % 4
        for h in range(2):
            to_y = 2 * (d % 2) + h
            source = wb.at[tile, h]
            target = b0.at[d // 2, y, core, x // 2, :, x % 2]
            mine = jnp.logical_and(to_y == y, tile // 4 == x)

            @pl.when(mine)
            def _():
                pltpu.make_async_copy(source, target, b2_recv.at[d // 2]).start()

            @pl.when(jnp.logical_not(mine))
            def _():
                remote(source, target, b2_send, b2_recv.at[d // 2],
                       device(to_y, core, tile // 4, z)).start()
        for k in range(1, 4):
            to = (z + k) % 4
            for e in range(2):
                remote(a_out.at[to, e, tile], a0.at[e, tile, z], a2_send, a2_recv.at[e, z],
                       device(y, core, x, to)).start()

    for e in range(2):
        pltpu.make_async_copy(
            a_out.at[z, e], a0.at[e, pl.ds(0, TILES), z], a2_recv.at[e, z]
        ).start()

    def left_half(stage, e):
        return lefts[stage].at[e, pl.ds(0, TILES)]

    def right_half(stage, e):
        return rights[stage].at[e, :, core]

    def source_of(stage, e):
        return (0, e) if stage == 1 else (0, 1 - e) if stage == 2 else (1, e)

    def left_copy(stage, e):
        return remote(
            left_half(*source_of(stage, e)), left_half(stage, e),
            a3_send.at[stage - 1, e], a3_recv.at[stage - 1, e],
            device(y, core, (x + 1 + 2 * e) % 4, z),
        )

    def right_copy(stage, e):
        return remote(
            right_half(*source_of(stage, e)), right_half(stage, e),
            b3_send.at[stage - 1, e], b3_recv.at[stage - 1, e],
            device((y + 1 + 2 * e) % 4, core, x, z),
        )

    def sibling_copy(stage, e):
        return remote(
            right_half(stage, e), right_half(stage, e),
            s_send.at[stage, e], s_recv.at[stage, e], device(y, 1 - core, x, z),
        )

    def offset(stage, e):
        return 0 if stage == 0 else 2 if stage == 3 else 3 - 2 * e

    def half_of(stage, e):
        return 1 - e if stage == 2 else e

    def units(left_stage, right_stage):
        @pl.loop(0, 4)
        def _(step):
            ea, eb = step // 2, step % 2
            piece = (x + offset(left_stage, ea)) % 4
            half = half_of(left_stage, ea)
            yy = (y + offset(right_stage, eb)) % 4
            d = 2 * half_of(right_stage, eb) + yy // 2
            column = (z - d + 4) % 4
            used = lens_s[column, piece // 2, 0]
            total = None
            for slot in range(SLOTS):
                inner = lists[piece // 2, slot, x * 4 + column]
                left = lefts[left_stage][ea, jnp.where(slot < used, inner, TILES)].reshape(128, 256)
                right = rights[right_stage][eb, inner // 4, inner // 2 % 2, inner % 2].reshape(256, 256)
                upper = jnp.concatenate([left[:, 128:], -left[:, :128]], axis=1)
                wide = jnp.concatenate([upper, left], axis=0)
                term = jnp.dot(wide, right, preferred_element_type=F32)
                total = term if total is None else total + term
            place = (left_stage * 4 + right_stage) * 4 + step
            c_out[place] = total.astype(BF16).reshape(2, 4, 32, 256)
            columns = pl.ds(pl.multiple_of(yy % 2 * 256, 256), 256)
            target = c_in.at[d, :, piece, :, half, :, columns]

            @pl.when(d == 0)
            def _():
                pltpu.make_async_copy(c_out.at[place], target, c_recv.at[0]).start()

            @pl.when(d != 0)
            def _():
                remote(c_out.at[place], target, c_send, c_recv.at[d],
                       device(y, core, x, column)).start()

    for e in range(2):
        wait_on(right_half(0, e), b2_recv.at[e])
        right_copy(1, e).start()
        sibling_copy(0, e).start()
    for e in range(2):
        for part in range(4):
            wait_on(a0.at[e, pl.ds(0, TILES), part], a2_recv.at[e, part])
        left_copy(1, e).start()
    for e in range(2):
        right_copy(2, e).start()
        left_copy(2, e).start()

    for k in range(1, 4):
        length_copies[k - 1].wait_recv()
    pltpu.make_async_copy(lens_all, lens_s, l_copy.at[1]).start()
    pltpu.make_async_copy(lens_all, lens_s, l_copy.at[1]).wait()
    list_copy.wait()

    for e in range(2):
        sibling_copy(0, e).wait_recv()
    units(0, 0)
    for stage in range(1, 4):
        for e in range(2):
            wait_on(right_half(stage, e), b3_recv.at[stage - 1, e])
            sibling_copy(stage, e).start()
            if stage == 1:
                right_copy(3, e).start()
        for e in range(2):
            wait_on(left_half(stage, e), a3_recv.at[stage - 1, e])
            if stage == 1:
                left_copy(3, e).start()
        for earlier in range(stage):
            units(stage, earlier)
        for e in range(2):
            sibling_copy(stage, e).wait_recv()
        for earlier in range(stage + 1):
            units(earlier, stage)

    wait_on(xt.at[pl.ds(0, DEVICES - 1)], p1_send)
    wait_on(wb.at[pl.ds(0, TILES - 1)], b2_send)
    wait_on(a_out.at[pl.ds(0, 3)], a2_send)
    for copy in length_copies:
        copy.wait_send()
    for e in range(2):
        for stage in range(4):
            sibling_copy(stage, e).wait_send()
        for stage in range(1, 4):
            left_copy(stage, e).wait_send()
            right_copy(stage, e).wait_send()
    wait_on(c_out.at[pl.ds(0, 48)], c_send)
    for d in range(4):
        wait_on(c_in.at[d], c_recv.at[d])


def local(data, fill_mask, obliquity, aperture, lengths):
    vmem = pl.BlockSpec(memory_space=pltpu.VMEM)
    far = pl.BlockSpec(memory_space=pl.ANY)
    dma = pltpu.SemaphoreType.DMA
    sums = pl.pallas_call(
        kernel,
        out_shape=jax.ShapeDtypeStruct((4, 2, 4, 4, 2, 32, TILE), BF16),
        in_specs=[vmem, vmem, vmem, vmem, far],
        out_specs=far,
        scratch_shapes=[
            pltpu.VMEM((DEVICES, ROWS, 128), BF16),
            pltpu.VMEM((DEVICES, ROWS, 128), BF16),
            pltpu.VMEM((TILES, 2, 2, ROWS, 256), BF16),
            pltpu.VMEM((4, 2, TILES, 32, 256), BF16),
        ]
        + [pltpu.VMEM((2, TILES + 1, 4, 32, 256), BF16)] * 4
        + [pltpu.VMEM((2, 4, 2, 2, 2, 2, ROWS, 256), BF16)] * 4
        + [
            pltpu.VMEM((64, 2, 4, 32, 256), BF16),
            pltpu.VMEM((8, 128), jnp.int32),
            pltpu.VMEM((4, 8, 128), jnp.int32),
            pltpu.SMEM((4, 8, 128), jnp.int32),
            pltpu.SMEM((2, SLOTS, TILES), jnp.int32),
            dma(()), dma((16,)), dma((3,)), dma((3,)), dma((2,)), dma(()), dma((2, 4)), dma(()), dma((2,)),
            dma((3, 2)), dma((3, 2)), dma((3, 2)), dma((3, 2)), dma((4, 2)), dma((4, 2)), dma(()), dma((4,)),
        ],
        compiler_params=pltpu.CompilerParams(
            has_side_effects=True, vmem_limit_bytes=63 * 1024 * 1024
        ),
        cost_estimate=pl.CostEstimate(
            flops=17_000_000_000, bytes_accessed=12_000_000, transcendentals=0
        ),
    )(data, fill_mask, obliquity.reshape(64, 128), lengths.T, jnp.swapaxes(aperture, 1, 2))
    total = sums[0].astype(F32)
    for d in range(1, 4):
        total = total + sums[d].astype(F32)
    return total.reshape(2, 2 * TILE, TILE)


def solution(mesh):
    placed = (
        P(None, ("src", "rcv"), None),
        P(("src", "rcv"), None),
        P(),
        P("src", None, None),
        P("src", "rcv"),
    )
    return jax.shard_map(
        local, mesh=mesh, in_specs=placed, out_specs=P(None, "src", "rcv"), check_vma=False
    )
```

```python
import jax
import jax.numpy as jnp
from jax import lax
from jax.experimental import pallas as pl
from jax.experimental.pallas import tpu as pltpu
from jax.sharding import PartitionSpec as P

TILE = 512
SLOTS = 8
TILES = 16
ROWS = 64
DEVICES = 128
MESH = pl.DeviceIdType.MESH
F32 = jnp.float32
BF16 = jnp.bfloat16


def kernel(
    data_far, mask_far, gain, lens, aperture,
    c_in,
    data, mask, xt, recv, wb, a_out, a0, a1, a2, a3, b0, b1, b2, b3, c_out, lens_own, lens_all, lens_s, lists,
    p1_send, p1_recv, l_send, l_recv, l_copy, a2_send, a2_recv, b2_send, b2_recv,
    a3_send, a3_recv, b3_send, b3_recv, s_send, s_recv, c_send, c_recv, in_copy, met,
):
    src, rcv = lax.axis_index("src"), lax.axis_index("rcv")
    y, core = src // 2, src % 2
    x, z = rcv // 4, rcv % 4
    me = src * 16 + rcv
    lefts = (a0, a1, a2, a3)
    rights = (b0, b1, b2, b3)

    def device(yy, cc, xx, zz):
        return (yy * 2 + cc, xx * 4 + zz)

    def remote(source, target, send, got, to):
        return pltpu.make_async_remote_copy(
            src_ref=source, dst_ref=target, send_sem=send, recv_sem=got,
            device_id=to, device_id_type=MESH,
        )

    def wait_on(ref, sem):
        pltpu.make_async_copy(ref, ref, sem).wait()

    data_copy = pltpu.make_async_copy(data_far, data, in_copy.at[0])
    mask_copy = pltpu.make_async_copy(mask_far, mask, in_copy.at[1])
    list_copy = pltpu.make_async_copy(aperture, lists, l_copy.at[0])
    data_copy.start()
    mask_copy.start()
    list_copy.start()

    barrier = pltpu.get_barrier_semaphore()
    along_x = [device(y, core, (x + k) % 4, z) for k in range(1, 4)]
    along_y = [device((y + k) % 4, core, x, z) for k in range(1, 4)]
    along_z = [device(y, core, x, (z + k) % 4) for k in range(1, 4)]
    sibling = [device(y, 1 - core, x, z)]

    def tell(semaphore, others):
        for other in others:
            pl.semaphore_signal(semaphore, inc=1, device_id=other, device_id_type=MESH)

    def turn(first, last):
        @pl.loop(first, last)
        def _(step):
            for i in range(2):
                q = step * 2 + i
                block = data[:, :, pl.ds(pl.multiple_of(q * 256, 256), 256)].reshape(128, 256)
                xt[pl.ds(q * 4, 4)] = block.T.reshape(4, ROWS, 128)

    tell(barrier, along_x + along_y + along_z + sibling)
    data_copy.wait()
    turn(0, 4)
    pl.semaphore_wait(barrier, 10)
    tell(met.at[0], along_x)
    turn(4, 8)
    pl.semaphore_wait(met.at[0], 3)
    tell(met.at[1], along_y)
    turn(8, 12)
    pl.semaphore_wait(met.at[1], 3)
    tell(met.at[2], sibling)
    turn(12, 16)
    pl.semaphore_wait(met.at[2], 1)

    def block_copy(target):
        return remote(xt.at[target], recv.at[me], p1_send, p1_recv.at[me // 8],
                      (target // 16, target % 16))

    pltpu.make_async_copy(xt.at[me], recv.at[me], p1_recv.at[me // 8]).start()
    for i in range(1, 4):
        block_copy(me // 4 * 4 + (me + i) % 4).start()

    @pl.loop(1, 32)
    def _(k):
        q = (me // 4 + k) % 32
        for i in range(4):
            block_copy(q * 4 + (me + i) % 4).start()

    lens_own[0:1, :] = jnp.broadcast_to(lens[:, 0:1], (1, 128))
    lens_own[1:2, :] = jnp.broadcast_to(lens[:, 1:2], (1, 128))
    lens_own[2:8, :] = jnp.zeros((6, 128), jnp.int32)
    lens_all[z] = lens_own[...]
    length_copies = []
    for k in range(1, 4):
        copy = remote(lens_own, lens_all.at[z], l_send.at[k - 1], l_recv.at[k - 1],
                      device(y, core, x, (z + k) % 4))
        copy.start()
        length_copies.append(copy)

    for buf in lefts:
        for e in range(2):
            buf[e, TILES] = jnp.zeros((4, 32, 256), BF16)

    lane = lax.broadcasted_iota(jnp.int32, (ROWS, 128), 1)
    low = lane < ROWS
    row = lax.broadcasted_iota(jnp.int32, (ROWS, 128), 0)
    gain_row = jnp.broadcast_to(gain[pl.ds(me // 2, 1), :], (ROWS, 128))
    gains = jnp.sum(
        jnp.where(lane == row + (me % 2) * ROWS, gain_row, 0.0), axis=1, keepdims=True
    )

    def join(first, second):
        return jnp.where(low, first, second)

    def swap(value):
        return pltpu.roll(value, ROWS, 1)

    mask_copy.wait()

    @pl.loop(0, TILES)
    def _(step):
        tile = (me // 8 - step - 1 + x % 2 + TILES) % TILES
        group = recv.at[pl.ds(tile * 8, 8)]
        wait_on(group, p1_recv.at[tile])
        filled = []
        for q in range(4):
            columns = pl.ds(pl.multiple_of(tile * 512 + q * 128, 128), 128)
            first = recv[tile * 8 + 2 * q].astype(F32)
            second = recv[tile * 8 + 2 * q + 1].astype(F32)
            turned = (join(first, swap(second)), join(swap(first), second))
            keep = mask[:, columns] == 1
            pair = []
            for part in range(2):
                value = jnp.where(keep, data[part, :, columns].astype(F32), turned[part])
                weighted = (value * gains).astype(BF16)
                wb[tile, q // 2, part, :, q % 2 * 128:(q % 2 + 1) * 128] = weighted
                pair.append(value)
            filled.append(pair)
        for part in range(2):
            lanes = slice((1 - part) * 128, (2 - part) * 128)
            for half in range(2):
                first, second = filled[half][part], filled[2 + half][part]
                for odd, value in ((0, join(first, swap(second))), (1, join(swap(first), second))):
                    value = (-value).astype(BF16)
                    a_out[2 * half + odd, 0, tile, :, lanes] = value[:32]
                    a_out[2 * half + odd, 1, tile, :, lanes] = value[32:]

        d = (z - tile % 4 + 4) % 4
        for h in range(2):
            to_y = 2 * (d % 2) + h
            source = wb.at[tile, h]
            target = b0.at[d // 2, y, core, x // 2, :, x % 2]
            mine = jnp.logical_and(to_y == y, tile // 4 == x)

            @pl.when(mine)
            def _():
                pltpu.make_async_copy(source, target, b2_recv.at[d // 2]).start()

            @pl.when(jnp.logical_not(mine))
            def _():
                remote(source, target, b2_send, b2_recv.at[d // 2],
                       device(to_y, core, tile // 4, z)).start()
        for k in range(1, 4):
            to = (z + k) % 4
            for e in range(2):
                remote(a_out.at[to, e, tile], a0.at[e, tile, z], a2_send, a2_recv.at[e, z],
                       device(y, core, x, to)).start()

    for e in range(2):
        pltpu.make_async_copy(
            a_out.at[z, e], a0.at[e, pl.ds(0, TILES), z], a2_recv.at[e, z]
        ).start()

    def left_half(stage, e):
        return lefts[stage].at[e, pl.ds(0, TILES)]

    def right_half(stage, e):
        return rights[stage].at[e, :, core]

    def source_of(stage, e):
        return (0, e) if stage == 1 else (0, 1 - e) if stage == 2 else (1, e)

    def left_copy(stage, e):
        return remote(
            left_half(*source_of(stage, e)), left_half(stage, e),
            a3_send.at[stage - 1, e], a3_recv.at[stage - 1, e],
            device(y, core, (x + 1 + 2 * e) % 4, z),
        )

    def right_copy(stage, e):
        return remote(
            right_half(*source_of(stage, e)), right_half(stage, e),
            b3_send.at[stage - 1, e], b3_recv.at[stage - 1, e],
            device((y + 1 + 2 * e) % 4, core, x, z),
        )

    def sibling_copy(stage, e):
        return remote(
            right_half(stage, e), right_half(stage, e),
            s_send.at[stage, e], s_recv.at[stage, e], device(y, 1 - core, x, z),
        )

    def offset(stage, e):
        return 0 if stage == 0 else 2 if stage == 3 else 3 - 2 * e

    def half_of(stage, e):
        return 1 - e if stage == 2 else e

    def units(left_stage, right_stage):
        @pl.loop(0, 4)
        def _(step):
            ea, eb = step // 2, step % 2
            piece = (x + offset(left_stage, ea)) % 4
            half = half_of(left_stage, ea)
            yy = (y + offset(right_stage, eb)) % 4
            d = 2 * half_of(right_stage, eb) + yy // 2
            column = (z - d + 4) % 4
            used = lens_s[column, piece // 2, 0]
            total = None
            for slot in range(SLOTS):
                inner = lists[piece // 2, slot, x * 4 + column]
                left = lefts[left_stage][ea, jnp.where(slot < used, inner, TILES)].reshape(128, 256)
                right = rights[right_stage][eb, inner // 4, inner // 2 % 2, inner % 2].reshape(256, 256)
                upper = jnp.concatenate([left[:, 128:], -left[:, :128]], axis=1)
                wide = jnp.concatenate([upper, left], axis=0)
                term = jnp.dot(wide, right, preferred_element_type=F32)
                total = term if total is None else total + term
            place = (left_stage * 4 + right_stage) * 4 + step
            c_out[place] = total.astype(BF16).reshape(2, 4, 32, 256)
            columns = pl.ds(pl.multiple_of(yy % 2 * 256, 256), 256)
            target = c_in.at[d, :, piece, :, half, :, columns]

            @pl.when(d == 0)
            def _():
                pltpu.make_async_copy(c_out.at[place], target, c_recv.at[0]).start()

            @pl.when(d != 0)
            def _():
                remote(c_out.at[place], target, c_send, c_recv.at[d],
                       device(y, core, x, column)).start()

    for e in range(2):
        wait_on(right_half(0, e), b2_recv.at[e])
        right_copy(1, e).start()
        sibling_copy(0, e).start()
    for e in range(2):
        for part in range(4):
            wait_on(a0.at[e, pl.ds(0, TILES), part], a2_recv.at[e, part])
        left_copy(1, e).start()
    for e in range(2):
        right_copy(2, e).start()
        left_copy(2, e).start()

    for k in range(1, 4):
        length_copies[k - 1].wait_recv()
    pltpu.make_async_copy(lens_all, lens_s, l_copy.at[1]).start()
    pltpu.make_async_copy(lens_all, lens_s, l_copy.at[1]).wait()
    list_copy.wait()

    for e in range(2):
        sibling_copy(0, e).wait_recv()
    units(0, 0)
    for stage in range(1, 4):
        for e in range(2):
            wait_on(right_half(stage, e), b3_recv.at[stage - 1, e])
            sibling_copy(stage, e).start()
            if stage == 1:
                right_copy(3, e).start()
        for e in range(2):
            wait_on(left_half(stage, e), a3_recv.at[stage - 1, e])
            if stage == 1:
                left_copy(3, e).start()
        for earlier in range(stage):
            units(stage, earlier)
        for e in range(2):
            sibling_copy(stage, e).wait_recv()
        for earlier in range(stage + 1):
            units(earlier, stage)

    wait_on(xt.at[pl.ds(0, DEVICES - 1)], p1_send)
    wait_on(wb.at[pl.ds(0, TILES - 1)], b2_send)
    wait_on(a_out.at[pl.ds(0, 3)], a2_send)
    for copy in length_copies:
        copy.wait_send()
    for e in range(2):
        for stage in range(4):
            sibling_copy(stage, e).wait_send()
        for stage in range(1, 4):
            left_copy(stage, e).wait_send()
            right_copy(stage, e).wait_send()
    wait_on(c_out.at[pl.ds(0, 48)], c_send)
    for d in range(4):
        wait_on(c_in.at[d], c_recv.at[d])


def local(data, fill_mask, obliquity, aperture, lengths):
    vmem = pl.BlockSpec(memory_space=pltpu.VMEM)
    far = pl.BlockSpec(memory_space=pl.ANY)
    dma = pltpu.SemaphoreType.DMA
    sums = pl.pallas_call(
        kernel,
        out_shape=jax.ShapeDtypeStruct((4, 2, 4, 4, 2, 32, TILE), BF16),
        in_specs=[far, far, vmem, vmem, far],
        out_specs=far,
        scratch_shapes=[
            pltpu.VMEM(data.shape, BF16),
            pltpu.VMEM(fill_mask.shape, jnp.int32),
            pltpu.VMEM((DEVICES, ROWS, 128), BF16),
            pltpu.VMEM((DEVICES, ROWS, 128), BF16),
            pltpu.VMEM((TILES, 2, 2, ROWS, 256), BF16),
            pltpu.VMEM((4, 2, TILES, 32, 256), BF16),
        ]
        + [pltpu.VMEM((2, TILES + 1, 4, 32, 256), BF16)] * 4
        + [pltpu.VMEM((2, 4, 2, 2, 2, 2, ROWS, 256), BF16)] * 4
        + [
            pltpu.VMEM((64, 2, 4, 32, 256), BF16),
            pltpu.VMEM((8, 128), jnp.int32),
            pltpu.VMEM((4, 8, 128), jnp.int32),
            pltpu.SMEM((4, 8, 128), jnp.int32),
            pltpu.SMEM((2, SLOTS, TILES), jnp.int32),
            dma(()), dma((16,)), dma((3,)), dma((3,)), dma((2,)), dma(()), dma((2, 4)), dma(()), dma((2,)),
            dma((3, 2)), dma((3, 2)), dma((3, 2)), dma((3, 2)), dma((4, 2)), dma((4, 2)), dma(()), dma((4,)),
            dma((2,)), pltpu.SemaphoreType.REGULAR((3,)),
        ],
        compiler_params=pltpu.CompilerParams(
            collective_id=1, has_side_effects=True, vmem_limit_bytes=63 * 1024 * 1024
        ),
        cost_estimate=pl.CostEstimate(
            flops=17_000_000_000, bytes_accessed=12_000_000, transcendentals=0
        ),
    )(data, fill_mask, obliquity.reshape(64, 128), lengths.T, jnp.swapaxes(aperture, 1, 2))
    total = sums[0].astype(F32)
    for d in range(1, 4):
        total = total + sums[d].astype(F32)
    return total.reshape(2, 2 * TILE, TILE)


def solution(mesh):
    placed = (
        P(None, ("src", "rcv"), None),
        P(("src", "rcv"), None),
        P(),
        P("src", None, None),
        P("src", "rcv"),
    )
    return jax.shard_map(
        local, mesh=mesh, in_specs=placed, out_specs=P(None, "src", "rcv"), check_vma=False
    )
```

```python
import jax
import jax.numpy as jnp
from jax import lax
from jax.experimental import pallas as pl
from jax.experimental.pallas import tpu as pltpu
from jax.sharding import PartitionSpec as P

TILE = 512
SLOTS = 8
TILES = 16
ROWS = 64
DEVICES = 128
MESH = pl.DeviceIdType.MESH
F32 = jnp.float32
BF16 = jnp.bfloat16


def kernel(
    data_far, mask_far, gain, lens, aperture,
    c_in,
    data, mask, xt, recv, wb, a_out, a0, a1, a2, a3, b0, b1, b2, b3, c_out, relay, lens_own, lens_all, lens_s, lists,
    p1_send, p1_recv, l_send, l_recv, l_copy, a2_send, a2_recv, b2_send, b2_recv,
    a3_send, a3_recv, b3_send, b3_recv, s_send, s_recv, c_send, c_recv, r_recv, in_copy, met,
):
    src, rcv = lax.axis_index("src"), lax.axis_index("rcv")
    y, core = src // 2, src % 2
    x, z = rcv // 4, rcv % 4
    me = src * 16 + rcv
    lefts = (a0, a1, a2, a3)
    rights = (b0, b1, b2, b3)

    def device(yy, cc, xx, zz):
        return (yy * 2 + cc, xx * 4 + zz)

    def remote(source, target, send, got, to):
        return pltpu.make_async_remote_copy(
            src_ref=source, dst_ref=target, send_sem=send, recv_sem=got,
            device_id=to, device_id_type=MESH,
        )

    def wait_on(ref, sem):
        pltpu.make_async_copy(ref, ref, sem).wait()

    data_copy = pltpu.make_async_copy(data_far, data, in_copy.at[0])
    mask_copy = pltpu.make_async_copy(mask_far, mask, in_copy.at[1])
    list_copy = pltpu.make_async_copy(aperture, lists, l_copy.at[0])
    data_copy.start()
    mask_copy.start()
    list_copy.start()

    barrier = pltpu.get_barrier_semaphore()
    along_x = [device(y, core, (x + k) % 4, z) for k in range(1, 4)]
    along_y = [device((y + k) % 4, core, x, z) for k in range(1, 4)]
    along_z = [device(y, core, x, (z + k) % 4) for k in range(1, 4)]
    sibling = [device(y, 1 - core, x, z)]

    def tell(semaphore, others):
        for other in others:
            pl.semaphore_signal(semaphore, inc=1, device_id=other, device_id_type=MESH)

    def turn(first, last):
        @pl.loop(first, last)
        def _(step):
            for i in range(2):
                q = step * 2 + i
                block = data[:, :, pl.ds(pl.multiple_of(q * 256, 256), 256)].reshape(128, 256)
                xt[pl.ds(q * 4, 4)] = block.T.reshape(4, ROWS, 128)

    tell(barrier, along_x + along_y + along_z + sibling)
    data_copy.wait()
    turn(0, 4)
    pl.semaphore_wait(barrier, 10)
    tell(met.at[0], along_x)
    turn(4, 8)
    pl.semaphore_wait(met.at[0], 3)
    tell(met.at[1], along_y)
    turn(8, 12)
    pl.semaphore_wait(met.at[1], 3)
    tell(met.at[2], sibling)
    turn(12, 16)
    pl.semaphore_wait(met.at[2], 1)

    def block_copy(target):
        return remote(xt.at[target], recv.at[me], p1_send, p1_recv.at[me // 8],
                      (target // 16, target % 16))

    pltpu.make_async_copy(xt.at[me], recv.at[me], p1_recv.at[me // 8]).start()
    for i in range(1, 4):
        block_copy(me // 4 * 4 + (me + i) % 4).start()

    @pl.loop(1, 32)
    def _(k):
        q = (me // 4 + k) % 32
        for i in range(4):
            block_copy(q * 4 + (me + i) % 4).start()

    lens_own[0:1, :] = jnp.broadcast_to(lens[:, 0:1], (1, 128))
    lens_own[1:2, :] = jnp.broadcast_to(lens[:, 1:2], (1, 128))
    lens_own[2:8, :] = jnp.zeros((6, 128), jnp.int32)
    lens_all[z] = lens_own[...]
    length_copies = []
    for k in range(1, 4):
        copy = remote(lens_own, lens_all.at[z], l_send.at[k - 1], l_recv.at[k - 1],
                      device(y, core, x, (z + k) % 4))
        copy.start()
        length_copies.append(copy)

    for buf in lefts:
        for e in range(2):
            buf[e, TILES] = jnp.zeros((4, 32, 256), BF16)

    lane = lax.broadcasted_iota(jnp.int32, (ROWS, 128), 1)
    low = lane < ROWS
    row = lax.broadcasted_iota(jnp.int32, (ROWS, 128), 0)
    gain_row = jnp.broadcast_to(gain[pl.ds(me // 2, 1), :], (ROWS, 128))
    gains = jnp.sum(
        jnp.where(lane == row + (me % 2) * ROWS, gain_row, 0.0), axis=1, keepdims=True
    )

    def join(first, second):
        return jnp.where(low, first, second)

    def swap(value):
        return pltpu.roll(value, ROWS, 1)

    mask_copy.wait()

    @pl.loop(0, TILES)
    def _(step):
        tile = (me // 8 - step - 1 + x % 2 + TILES) % TILES
        group = recv.at[pl.ds(tile * 8, 8)]
        wait_on(group, p1_recv.at[tile])
        filled = []
        for q in range(4):
            columns = pl.ds(pl.multiple_of(tile * 512 + q * 128, 128), 128)
            first = recv[tile * 8 + 2 * q].astype(F32)
            second = recv[tile * 8 + 2 * q + 1].astype(F32)
            turned = (join(first, swap(second)), join(swap(first), second))
            keep = mask[:, columns] == 1
            pair = []
            for part in range(2):
                value = jnp.where(keep, data[part, :, columns].astype(F32), turned[part])
                weighted = (value * gains).astype(BF16)
                wb[tile, q // 2, part, :, q % 2 * 128:(q % 2 + 1) * 128] = weighted
                pair.append(value)
            filled.append(pair)
        for part in range(2):
            lanes = slice((1 - part) * 128, (2 - part) * 128)
            for half in range(2):
                first, second = filled[half][part], filled[2 + half][part]
                for odd, value in ((0, join(first, swap(second))), (1, join(swap(first), second))):
                    value = (-value).astype(BF16)
                    a_out[2 * half + odd, 0, tile, :, lanes] = value[:32]
                    a_out[2 * half + odd, 1, tile, :, lanes] = value[32:]

        d = (z - tile % 4 + 4) % 4
        for h in range(2):
            to_y = 2 * (d % 2) + h
            source = wb.at[tile, h]
            target = b0.at[d // 2, y, core, x // 2, :, x % 2]
            mine = jnp.logical_and(to_y == y, tile // 4 == x)

            @pl.when(mine)
            def _():
                pltpu.make_async_copy(source, target, b2_recv.at[d // 2]).start()

            @pl.when(jnp.logical_not(mine))
            def _():
                remote(source, target, b2_send, b2_recv.at[d // 2],
                       device(to_y, core, tile // 4, z)).start()
        for k in range(1, 4):
            to = (z + k) % 4
            for e in range(2):
                remote(a_out.at[to, e, tile], a0.at[e, tile, z], a2_send, a2_recv.at[e, z],
                       device(y, core, x, to)).start()

    for e in range(2):
        pltpu.make_async_copy(
            a_out.at[z, e], a0.at[e, pl.ds(0, TILES), z], a2_recv.at[e, z]
        ).start()

    def left_half(stage, e):
        return lefts[stage].at[e, pl.ds(0, TILES)]

    def right_half(stage, e):
        return rights[stage].at[e, :, core]

    def source_of(stage, e):
        return (0, e) if stage == 1 else (0, 1 - e) if stage == 2 else (1, e)

    def left_copy(stage, e):
        return remote(
            left_half(*source_of(stage, e)), left_half(stage, e),
            a3_send.at[stage - 1, e], a3_recv.at[stage - 1, e],
            device(y, core, (x + 1 + 2 * e) % 4, z),
        )

    def right_copy(stage, e):
        return remote(
            right_half(*source_of(stage, e)), right_half(stage, e),
            b3_send.at[stage - 1, e], b3_recv.at[stage - 1, e],
            device((y + 1 + 2 * e) % 4, core, x, z),
        )

    def sibling_copy(stage, e):
        return remote(
            right_half(stage, e), right_half(stage, e),
            s_send.at[stage, e], s_recv.at[stage, e], device(y, 1 - core, x, z),
        )

    def offset(stage, e):
        return 0 if stage == 0 else 2 if stage == 3 else 3 - 2 * e

    def half_of(stage, e):
        return 1 - e if stage == 2 else e

    def units(left_stage, right_stage):
        @pl.loop(0, 4)
        def _(step):
            ea, eb = step // 2, step % 2
            piece = (x + offset(left_stage, ea)) % 4
            half = half_of(left_stage, ea)
            yy = (y + offset(right_stage, eb)) % 4
            d = 2 * half_of(right_stage, eb) + yy // 2
            column = (z - d + 4) % 4
            used = lens_s[column, piece // 2, 0]
            total = None
            for slot in range(SLOTS):
                inner = lists[piece // 2, slot, x * 4 + column]
                left = lefts[left_stage][ea, jnp.where(slot < used, inner, TILES)].reshape(128, 256)
                right = rights[right_stage][eb, inner // 4, inner // 2 % 2, inner % 2].reshape(256, 256)
                upper = jnp.concatenate([left[:, 128:], -left[:, :128]], axis=1)
                wide = jnp.concatenate([upper, left], axis=0)
                term = jnp.dot(wide, right, preferred_element_type=F32)
                total = term if total is None else total + term
            h = yy % 2
            index = left_stage * 2 + ea
            held = c_out.at[index, d, h]
            held[...] = total.astype(BF16).reshape(2, 4, 32, 256)
            target = sum_place(d, piece, half, h)

            @pl.when(d == 0)
            def _():
                pltpu.make_async_copy(held, target, c_recv.at[0]).start()

            @pl.when(d == 2)
            def _():
                for way in range(2):
                    remote(held.at[:, pl.ds(2 * way, 2)], relay.at[index, way, h],
                           c_send, r_recv.at[index, way, h],
                           device(y, core, x, (z + 3 - 2 * way) % 4)).start()

            @pl.when(d % 2 == 1)
            def _():
                rows = pl.ds(3 - d, 2)
                remote(held.at[:, rows], target.at[:, rows], c_send, c_recv.at[d // 2 + 1],
                       device(y, core, x, column)).start()

    def sum_place(d, piece, half, h):
        columns = pl.ds(pl.multiple_of(h * 256, 256), 256)
        return c_in.at[(d + 1) // 2, :, piece, :, half, :, columns]

    def finish(first, last, h):
        @pl.loop(2 * first, 2 * last)
        def _(step):
            index, way = step // 2, step % 2
            stage, e = index // 2, index % 2
            near = jnp.logical_or(stage == 1, stage == 2)
            piece = (x + jnp.where(near, 3 - 2 * e, stage // 3 * 2)) % 4
            half = jnp.where(stage == 2, 1 - e, e)
            d = 2 * way + 1
            wait_on(relay.at[index, way, h], r_recv.at[index, way, h])
            rows = pl.ds(2 * way, 2)
            held = c_out.at[index, d, h, :, rows]
            held[...] = (held[...].astype(F32) + relay[index, way, h].astype(F32)).astype(BF16)
            remote(held, sum_place(d, piece, half, h).at[:, rows], c_send, c_recv.at[way + 1],
                   device(y, core, x, (z - d + 4) % 4)).start()

    for e in range(2):
        wait_on(right_half(0, e), b2_recv.at[e])
        right_copy(1, e).start()
        sibling_copy(0, e).start()
    for e in range(2):
        for part in range(4):
            wait_on(a0.at[e, pl.ds(0, TILES), part], a2_recv.at[e, part])
        left_copy(1, e).start()
    for e in range(2):
        right_copy(2, e).start()
        left_copy(2, e).start()

    for k in range(1, 4):
        length_copies[k - 1].wait_recv()
    pltpu.make_async_copy(lens_all, lens_s, l_copy.at[1]).start()
    pltpu.make_async_copy(lens_all, lens_s, l_copy.at[1]).wait()
    list_copy.wait()

    for e in range(2):
        sibling_copy(0, e).wait_recv()
    units(0, 0)
    soon, late = 1 - y % 2, y % 2
    for stage in range(1, 4):
        for e in range(2):
            wait_on(right_half(stage, e), b3_recv.at[stage - 1, e])
            sibling_copy(stage, e).start()
            if stage == 1:
                right_copy(3, e).start()
        for e in range(2):
            wait_on(left_half(stage, e), a3_recv.at[stage - 1, e])
            if stage == 1:
                left_copy(3, e).start()
        units(stage, 0)
        if stage == 2:
            units(2, 1)
        for e in range(2):
            sibling_copy(stage, e).wait_recv()
        for earlier in range(stage):
            units(earlier, stage)
        if stage < 3:
            units(stage, stage)
        if stage == 2:
            finish(0, 6, soon)
    units(3, 1)
    finish(0, 6, late)
    units(3, 2)
    units(3, 3)
    finish(6, 8, soon)
    finish(6, 8, late)

    wait_on(xt.at[pl.ds(0, DEVICES - 1)], p1_send)
    wait_on(wb.at[pl.ds(0, TILES - 1)], b2_send)
    wait_on(a_out.at[pl.ds(0, 3)], a2_send)
    for copy in length_copies:
        copy.wait_send()
    for e in range(2):
        for stage in range(4):
            sibling_copy(stage, e).wait_send()
        for stage in range(1, 4):
            left_copy(stage, e).wait_send()
            right_copy(stage, e).wait_send()
    wait_on(c_out.at[pl.ds(0, 6)], c_send)
    for side in range(3):
        wait_on(c_in.at[side], c_recv.at[side])


def local(data, fill_mask, obliquity, aperture, lengths):
    vmem = pl.BlockSpec(memory_space=pltpu.VMEM)
    far = pl.BlockSpec(memory_space=pl.ANY)
    dma = pltpu.SemaphoreType.DMA
    sums = pl.pallas_call(
        kernel,
        out_shape=jax.ShapeDtypeStruct((3, 2, 4, 4, 2, 32, TILE), BF16),
        in_specs=[far, far, vmem, vmem, far],
        out_specs=far,
        scratch_shapes=[
            pltpu.VMEM(data.shape, BF16),
            pltpu.VMEM(fill_mask.shape, jnp.int32),
            pltpu.VMEM((DEVICES, ROWS, 128), BF16),
            pltpu.VMEM((DEVICES, ROWS, 128), BF16),
            pltpu.VMEM((TILES, 2, 2, ROWS, 256), BF16),
            pltpu.VMEM((4, 2, TILES, 32, 256), BF16),
        ]
        + [pltpu.VMEM((2, TILES + 1, 4, 32, 256), BF16)] * 4
        + [pltpu.VMEM((2, 4, 2, 2, 2, 2, ROWS, 256), BF16)] * 4
        + [
            pltpu.VMEM((8, 4, 2, 2, 4, 32, 256), BF16),
            pltpu.VMEM((8, 2, 2, 2, 2, 32, 256), BF16),
            pltpu.VMEM((8, 128), jnp.int32),
            pltpu.VMEM((4, 8, 128), jnp.int32),
            pltpu.SMEM((4, 8, 128), jnp.int32),
            pltpu.SMEM((2, SLOTS, TILES), jnp.int32),
            dma(()), dma((16,)), dma((3,)), dma((3,)), dma((2,)), dma(()), dma((2, 4)), dma(()), dma((2,)),
            dma((3, 2)), dma((3, 2)), dma((3, 2)), dma((3, 2)), dma((4, 2)), dma((4, 2)), dma(()), dma((3,)),
            dma((8, 2, 2)),
            dma((2,)), pltpu.SemaphoreType.REGULAR((3,)),
        ],
        compiler_params=pltpu.CompilerParams(
            collective_id=1, has_side_effects=True, vmem_limit_bytes=63 * 1024 * 1024
        ),
        cost_estimate=pl.CostEstimate(
            flops=17_000_000_000, bytes_accessed=12_000_000, transcendentals=0
        ),
    )(data, fill_mask, obliquity.reshape(64, 128), lengths.T, jnp.swapaxes(aperture, 1, 2))
    total = sums[0].astype(F32)
    for side in range(1, 3):
        total = total + sums[side].astype(F32)
    return total.reshape(2, 2 * TILE, TILE)


def solution(mesh):
    placed = (
        P(None, ("src", "rcv"), None),
        P(("src", "rcv"), None),
        P(),
        P("src", None, None),
        P("src", "rcv"),
    )
    return jax.shard_map(
        local, mesh=mesh, in_specs=placed, out_specs=P(None, "src", "rcv"), check_vma=False
    )
```

```python
import jax
import jax.numpy as jnp
from jax import lax
from jax.experimental import pallas as pl
from jax.experimental.pallas import tpu as pltpu
from jax.sharding import PartitionSpec as P

TILE = 512
SLOTS = 8
TILES = 16
ROWS = 64
DEVICES = 128
STRIDE = 5
MESH = pl.DeviceIdType.MESH
F32 = jnp.float32
BF16 = jnp.bfloat16


def kernel(
    data_far, mask_far, gain, lens, aperture,
    c_in,
    data, mask, xt, recv, wb, a_out, a0, a1, a2, a3, b0, b1, b2, b3, c_out, relay, lens_own, lens_all, lens_s, lists,
    p1_send, p1_recv, l_send, l_recv, l_copy, a2_send, a2_recv, b2_send, b2_recv,
    a3_send, a3_recv, b3_send, b3_recv, s_send, s_recv, c_send, c_recv, r_recv, in_copy, met,
):
    src, rcv = lax.axis_index("src"), lax.axis_index("rcv")
    y, core = src // 2, src % 2
    x, z = rcv // 4, rcv % 4
    me = src * 16 + rcv
    lefts = (a0, a1, a2, a3)
    rights = (b0, b1, b2, b3)

    def device(yy, cc, xx, zz):
        return (yy * 2 + cc, xx * 4 + zz)

    def remote(source, target, send, got, to):
        return pltpu.make_async_remote_copy(
            src_ref=source, dst_ref=target, send_sem=send, recv_sem=got,
            device_id=to, device_id_type=MESH,
        )

    def wait_on(ref, sem):
        pltpu.make_async_copy(ref, ref, sem).wait()

    data_copy = pltpu.make_async_copy(data_far, data, in_copy.at[0])
    mask_copy = pltpu.make_async_copy(mask_far, mask, in_copy.at[1])
    list_copy = pltpu.make_async_copy(aperture, lists, l_copy.at[0])
    data_copy.start()
    mask_copy.start()
    list_copy.start()

    barrier = pltpu.get_barrier_semaphore()

    def tell(semaphore, others):
        for other in others:
            pl.semaphore_signal(semaphore, inc=1, device_id=other, device_id_type=MESH)

    def turn(first, last):
        @pl.loop(first, last)
        def _(step):
            for i in range(2):
                q = step * 2 + i
                block = data[:, :, pl.ds(pl.multiple_of(q * 256, 256), 256)].reshape(128, 256)
                xt[pl.ds(q * 4, 4)] = block.T.reshape(4, ROWS, 128)

    along_yz = [device((y + k // 4) % 4, core, x, (z + k) % 4) for k in range(1, 16)]
    across = [device(y, (core + k // 4) % 2, (x + k) % 4, z) for k in range(1, 8)]
    tell(barrier, along_yz + across)
    data_copy.wait()
    turn(0, 8)
    pl.semaphore_wait(barrier, 22)
    tell(met, across)
    turn(8, 16)
    pl.semaphore_wait(met, 7)

    def block_copy(target):
        return remote(xt.at[target], recv.at[me], p1_send, p1_recv.at[me // 8],
                      (target // 16, target % 16))

    pltpu.make_async_copy(xt.at[me], recv.at[me], p1_recv.at[me // 8]).start()
    for i in range(1, 8):
        block_copy(me // 8 * 8 + (me + i) % 8).start()

    @pl.loop(1, TILES)
    def _(step):
        tile = (me // 8 + STRIDE * step) % TILES
        for i in range(8):
            block_copy(tile * 8 + (me + i) % 8).start()

    lens_own[0:1, :] = jnp.broadcast_to(lens[:, 0:1], (1, 128))
    lens_own[1:2, :] = jnp.broadcast_to(lens[:, 1:2], (1, 128))
    lens_own[2:8, :] = jnp.zeros((6, 128), jnp.int32)
    lens_all[z] = lens_own[...]
    length_copies = []
    for k in range(1, 4):
        copy = remote(lens_own, lens_all.at[z], l_send.at[k - 1], l_recv.at[k - 1],
                      device(y, core, x, (z + k) % 4))
        copy.start()
        length_copies.append(copy)

    for buf in lefts:
        for e in range(2):
            buf[e, TILES] = jnp.zeros((4, 32, 256), BF16)

    lane = lax.broadcasted_iota(jnp.int32, (ROWS, 128), 1)
    low = lane < ROWS
    row = lax.broadcasted_iota(jnp.int32, (ROWS, 128), 0)
    gain_row = jnp.broadcast_to(gain[pl.ds(me // 2, 1), :], (ROWS, 128))
    gains = jnp.sum(
        jnp.where(lane == row + (me % 2) * ROWS, gain_row, 0.0), axis=1, keepdims=True
    )

    def join(first, second):
        return jnp.where(low, first, second)

    def swap(value):
        return pltpu.roll(value, ROWS, 1)

    mask_copy.wait()

    @pl.loop(0, TILES)
    def _(step):
        tile = (me // 8 + (TILES - STRIDE) * step) % TILES
        group = recv.at[pl.ds(tile * 8, 8)]
        wait_on(group, p1_recv.at[tile])
        filled = []
        for q in range(4):
            columns = pl.ds(pl.multiple_of(tile * 512 + q * 128, 128), 128)
            first = recv[tile * 8 + 2 * q].astype(F32)
            second = recv[tile * 8 + 2 * q + 1].astype(F32)
            turned = (join(first, swap(second)), join(swap(first), second))
            keep = mask[:, columns] == 1
            pair = []
            for part in range(2):
                value = jnp.where(keep, data[part, :, columns].astype(F32), turned[part])
                weighted = (value * gains).astype(BF16)
                wb[tile, q // 2, part, :, q % 2 * 128:(q % 2 + 1) * 128] = weighted
                pair.append(value)
            filled.append(pair)
        for part in range(2):
            lanes = slice((1 - part) * 128, (2 - part) * 128)
            for half in range(2):
                first, second = filled[half][part], filled[2 + half][part]
                for odd, value in ((0, join(first, swap(second))), (1, join(swap(first), second))):
                    value = (-value).astype(BF16)
                    a_out[2 * half + odd, 0, tile, :, lanes] = value[:32]
                    a_out[2 * half + odd, 1, tile, :, lanes] = value[32:]

        d = (z - tile % 4 + 4) % 4
        for h in range(2):
            to_y = 2 * (d % 2) + h
            source = wb.at[tile, h]
            target = b0.at[d // 2, y, core, x // 2, :, x % 2]
            mine = jnp.logical_and(to_y == y, tile // 4 == x)

            @pl.when(mine)
            def _():
                pltpu.make_async_copy(source, target, b2_recv.at[d // 2]).start()

            @pl.when(jnp.logical_not(mine))
            def _():
                remote(source, target, b2_send, b2_recv.at[d // 2],
                       device(to_y, core, tile // 4, z)).start()
        for k in range(1, 4):
            to = (z + k) % 4
            for e in range(2):
                remote(a_out.at[to, e, tile], a0.at[e, tile, z], a2_send, a2_recv.at[e, z],
                       device(y, core, x, to)).start()

    for e in range(2):
        pltpu.make_async_copy(
            a_out.at[z, e], a0.at[e, pl.ds(0, TILES), z], a2_recv.at[e, z]
        ).start()

    def left_half(stage, e):
        return lefts[stage].at[e, pl.ds(0, TILES)]

    def right_half(stage, e):
        return rights[stage].at[e, :, core]

    def source_of(stage, e):
        return (0, e) if stage == 1 else (0, 1 - e) if stage == 2 else (1, e)

    def left_copy(stage, e):
        return remote(
            left_half(*source_of(stage, e)), left_half(stage, e),
            a3_send.at[stage - 1, e], a3_recv.at[stage - 1, e],
            device(y, core, (x + 1 + 2 * e) % 4, z),
        )

    def right_copy(stage, e):
        return remote(
            right_half(*source_of(stage, e)), right_half(stage, e),
            b3_send.at[stage - 1, e], b3_recv.at[stage - 1, e],
            device((y + 1 + 2 * e) % 4, core, x, z),
        )

    def sibling_copy(stage, e):
        return remote(
            right_half(stage, e), right_half(stage, e),
            s_send.at[stage, e], s_recv.at[stage, e], device(y, 1 - core, x, z),
        )

    def offset(stage, e):
        return 0 if stage == 0 else 2 if stage == 3 else 3 - 2 * e

    def half_of(stage, e):
        return 1 - e if stage == 2 else e

    def units(left_stage, right_stage):
        @pl.loop(0, 4)
        def _(step):
            ea, eb = step // 2, step % 2
            piece = (x + offset(left_stage, ea)) % 4
            half = half_of(left_stage, ea)
            yy = (y + offset(right_stage, eb)) % 4
            d = 2 * half_of(right_stage, eb) + yy // 2
            column = (z - d + 4) % 4
            used = lens_s[column, piece // 2, 0]
            total = None
            for slot in range(SLOTS):
                inner = lists[piece // 2, slot, x * 4 + column]
                left = lefts[left_stage][ea, jnp.where(slot < used, inner, TILES)].reshape(128, 256)
                right = rights[right_stage][eb, inner // 4, inner // 2 % 2, inner % 2].reshape(256, 256)
                upper = jnp.concatenate([left[:, 128:], -left[:, :128]], axis=1)
                wide = jnp.concatenate([upper, left], axis=0)
                term = jnp.dot(wide, right, preferred_element_type=F32)
                total = term if total is None else total + term
            h = yy % 2
            index = left_stage * 2 + ea
            held = c_out.at[index, d, h]
            held[...] = total.astype(BF16).reshape(2, 4, 32, 256)
            target = sum_place(d, piece, half, h)

            @pl.when(d == 0)
            def _():
                pltpu.make_async_copy(held, target, c_recv.at[0]).start()

            @pl.when(d == 2)
            def _():
                for way in range(2):
                    remote(held.at[:, pl.ds(2 * way, 2)], relay.at[index, way, h],
                           c_send, r_recv.at[index, way, h],
                           device(y, core, x, (z + 3 - 2 * way) % 4)).start()

            @pl.when(d % 2 == 1)
            def _():
                rows = pl.ds(3 - d, 2)
                remote(held.at[:, rows], target.at[:, rows], c_send, c_recv.at[d // 2 + 1],
                       device(y, core, x, column)).start()

    def sum_place(d, piece, half, h):
        columns = pl.ds(pl.multiple_of(h * 256, 256), 256)
        return c_in.at[(d + 1) // 2, :, piece, :, half, :, columns]

    def finish(first, last, h):
        @pl.loop(2 * first, 2 * last)
        def _(step):
            index, way = step // 2, step % 2
            stage, e = index // 2, index % 2
            near = jnp.logical_or(stage == 1, stage == 2)
            piece = (x + jnp.where(near, 3 - 2 * e, stage // 3 * 2)) % 4
            half = jnp.where(stage == 2, 1 - e, e)
            d = 2 * way + 1
            wait_on(relay.at[index, way, h], r_recv.at[index, way, h])
            rows = pl.ds(2 * way, 2)
            held = c_out.at[index, d, h, :, rows]
            held[...] = (held[...].astype(F32) + relay[index, way, h].astype(F32)).astype(BF16)
            remote(held, sum_place(d, piece, half, h).at[:, rows], c_send, c_recv.at[way + 1],
                   device(y, core, x, (z - d + 4) % 4)).start()

    for e in range(2):
        wait_on(right_half(0, e), b2_recv.at[e])
        right_copy(1, e).start()
        sibling_copy(0, e).start()
    for e in range(2):
        for part in range(4):
            wait_on(a0.at[e, pl.ds(0, TILES), part], a2_recv.at[e, part])
        left_copy(1, e).start()
    for e in range(2):
        right_copy(2, e).start()
        left_copy(2, e).start()

    for k in range(1, 4):
        length_copies[k - 1].wait_recv()
    pltpu.make_async_copy(lens_all, lens_s, l_copy.at[1]).start()
    pltpu.make_async_copy(lens_all, lens_s, l_copy.at[1]).wait()
    list_copy.wait()

    for e in range(2):
        sibling_copy(0, e).wait_recv()
    units(0, 0)
    soon, late = 1 - y % 2, y % 2
    for stage in range(1, 4):
        for e in range(2):
            wait_on(right_half(stage, e), b3_recv.at[stage - 1, e])
            sibling_copy(stage, e).start()
            if stage == 1:
                right_copy(3, e).start()
        for e in range(2):
            wait_on(left_half(stage, e), a3_recv.at[stage - 1, e])
            if stage == 1:
                left_copy(3, e).start()
        units(stage, 0)
        if stage == 2:
            units(2, 1)
        for e in range(2):
            sibling_copy(stage, e).wait_recv()
        for earlier in range(stage):
            units(earlier, stage)
        if stage < 3:
            units(stage, stage)
        if stage == 2:
            finish(0, 6, soon)
    units(3, 1)
    finish(0, 6, late)
    units(3, 2)
    units(3, 3)
    finish(6, 8, soon)
    finish(6, 8, late)

    wait_on(xt.at[pl.ds(0, DEVICES - 1)], p1_send)
    wait_on(wb.at[pl.ds(0, TILES - 1)], b2_send)
    wait_on(a_out.at[pl.ds(0, 3)], a2_send)
    for copy in length_copies:
        copy.wait_send()
    for e in range(2):
        for stage in range(4):
            sibling_copy(stage, e).wait_send()
        for stage in range(1, 4):
            left_copy(stage, e).wait_send()
            right_copy(stage, e).wait_send()
    wait_on(c_out.at[pl.ds(0, 6)], c_send)
    for side in range(3):
        wait_on(c_in.at[side], c_recv.at[side])


def local(data, fill_mask, obliquity, aperture, lengths):
    vmem = pl.BlockSpec(memory_space=pltpu.VMEM)
    far = pl.BlockSpec(memory_space=pl.ANY)
    dma = pltpu.SemaphoreType.DMA
    sums = pl.pallas_call(
        kernel,
        out_shape=pltpu.VMEM((3, 2, 4, 4, 2, 32, TILE), BF16),
        in_specs=[far, far, vmem, vmem, far],
        out_specs=vmem,
        scratch_shapes=[
            pltpu.VMEM(data.shape, BF16),
            pltpu.VMEM(fill_mask.shape, jnp.int32),
            pltpu.VMEM((DEVICES, ROWS, 128), BF16),
            pltpu.VMEM((DEVICES, ROWS, 128), BF16),
            pltpu.VMEM((TILES, 2, 2, ROWS, 256), BF16),
            pltpu.VMEM((4, 2, TILES, 32, 256), BF16),
        ]
        + [pltpu.VMEM((2, TILES + 1, 4, 32, 256), BF16)] * 4
        + [pltpu.VMEM((2, 4, 2, 2, 2, 2, ROWS, 256), BF16)] * 4
        + [
            pltpu.VMEM((8, 4, 2, 2, 4, 32, 256), BF16),
            pltpu.VMEM((8, 2, 2, 2, 2, 32, 256), BF16),
            pltpu.VMEM((8, 128), jnp.int32),
            pltpu.VMEM((4, 8, 128), jnp.int32),
            pltpu.SMEM((4, 8, 128), jnp.int32),
            pltpu.SMEM((2, SLOTS, TILES), jnp.int32),
            dma(()), dma((16,)), dma((3,)), dma((3,)), dma((2,)), dma(()), dma((2, 4)), dma(()), dma((2,)),
            dma((3, 2)), dma((3, 2)), dma((3, 2)), dma((3, 2)), dma((4, 2)), dma((4, 2)), dma(()), dma((3,)),
            dma((8, 2, 2)),
            dma((2,)), pltpu.SemaphoreType.REGULAR,
        ],
        compiler_params=pltpu.CompilerParams(
            collective_id=1, has_side_effects=True, vmem_limit_bytes=50 * 1024 * 1024
        ),
        cost_estimate=pl.CostEstimate(
            flops=17_000_000_000, bytes_accessed=12_000_000, transcendentals=0
        ),
    )(data, fill_mask, obliquity.reshape(64, 128), lengths.T, jnp.swapaxes(aperture, 1, 2))
    total = sums[0].astype(F32)
    for side in range(1, 3):
        total = total + sums[side].astype(F32)
    return total.reshape(2, 2 * TILE, TILE)


def solution(mesh):
    placed = (
        P(None, ("src", "rcv"), None),
        P(("src", "rcv"), None),
        P(),
        P("src", None, None),
        P("src", "rcv"),
    )
    return jax.shard_map(
        local, mesh=mesh, in_specs=placed, out_specs=P(None, "src", "rcv"), check_vma=False
    )
```

```python
import jax
import jax.numpy as jnp
from jax import lax
from jax.experimental import pallas as pl
from jax.experimental.pallas import tpu as pltpu
from jax.sharding import PartitionSpec as P

TILE = 512
SLOTS = 8
TILES = 16
ROWS = 64
DEVICES = 128
STRIDE = 5
MESH = pl.DeviceIdType.MESH
F32 = jnp.float32
BF16 = jnp.bfloat16


def kernel(
    data_far, mask_far, gain, lens, aperture,
    mine, c_in,
    data, mask, xt, recv, wb, a_out, a0, a1, a2, a3, b0, b1, b2, b3, c_out, relay, kept, lens_own, lens_all, lens_s, lists,
    p1_send, p1_recv, l_send, l_recv, l_copy, a2_send, a2_recv, b2_send, b2_recv,
    a3_send, a3_recv, b3_send, b3_recv, s_send, s_recv, c_send, c_recv, r_recv, in_copy, met,
):
    src, rcv = lax.axis_index("src"), lax.axis_index("rcv")
    y, core = src // 2, src % 2
    x, z = rcv // 4, rcv % 4
    me = src * 16 + rcv
    lefts = (a0, a1, a2, a3)
    rights = (b0, b1, b2, b3)

    def device(yy, cc, xx, zz):
        return (yy * 2 + cc, xx * 4 + zz)

    def remote(source, target, send, got, to):
        return pltpu.make_async_remote_copy(
            src_ref=source, dst_ref=target, send_sem=send, recv_sem=got,
            device_id=to, device_id_type=MESH,
        )

    def wait_on(ref, sem):
        pltpu.make_async_copy(ref, ref, sem).wait()

    data_copy = pltpu.make_async_copy(data_far, data, in_copy.at[0])
    mask_copy = pltpu.make_async_copy(mask_far, mask, in_copy.at[1])
    list_copy = pltpu.make_async_copy(aperture, lists, l_copy.at[0])
    data_copy.start()
    mask_copy.start()
    list_copy.start()

    barrier = pltpu.get_barrier_semaphore()

    def tell(semaphore, others):
        for other in others:
            pl.semaphore_signal(semaphore, inc=1, device_id=other, device_id_type=MESH)

    def turn(first, last):
        @pl.loop(first, last)
        def _(step):
            for i in range(2):
                q = step * 2 + i
                block = data[:, :, pl.ds(pl.multiple_of(q * 256, 256), 256)].reshape(128, 256)
                xt[pl.ds(q * 4, 4)] = block.T.reshape(4, ROWS, 128)

    along_yz = [device((y + k // 4) % 4, core, x, (z + k) % 4) for k in range(1, 16)]
    across = [device(y, (core + k // 4) % 2, (x + k) % 4, z) for k in range(1, 8)]
    tell(barrier, along_yz + across)
    data_copy.wait()
    turn(0, 8)
    pl.semaphore_wait(barrier, 22)
    tell(met, across)
    turn(8, 16)
    pl.semaphore_wait(met, 7)

    def block_copy(target):
        return remote(xt.at[target], recv.at[me], p1_send, p1_recv.at[me // 8],
                      (target // 16, target % 16))

    pltpu.make_async_copy(xt.at[me], recv.at[me], p1_recv.at[me // 8]).start()
    for i in range(1, 8):
        block_copy(me // 8 * 8 + (me + i) % 8).start()

    @pl.loop(1, TILES)
    def _(step):
        tile = (me // 8 + STRIDE * step) % TILES
        for i in range(8):
            block_copy(tile * 8 + (me + i) % 8).start()

    lens_own[0:1, :] = jnp.broadcast_to(lens[:, 0:1], (1, 128))
    lens_own[1:2, :] = jnp.broadcast_to(lens[:, 1:2], (1, 128))
    lens_own[2:8, :] = jnp.zeros((6, 128), jnp.int32)
    lens_all[z] = lens_own[...]
    length_copies = []
    for k in range(1, 4):
        copy = remote(lens_own, lens_all.at[z], l_send.at[k - 1], l_recv.at[k - 1],
                      device(y, core, x, (z + k) % 4))
        copy.start()
        length_copies.append(copy)

    for buf in lefts:
        for e in range(2):
            buf[e, TILES] = jnp.zeros((4, 32, 256), BF16)

    lane = lax.broadcasted_iota(jnp.int32, (ROWS, 128), 1)
    low = lane < ROWS
    row = lax.broadcasted_iota(jnp.int32, (ROWS, 128), 0)
    gain_row = jnp.broadcast_to(gain[pl.ds(me // 2, 1), :], (ROWS, 128))
    gains = jnp.sum(
        jnp.where(lane == row + (me % 2) * ROWS, gain_row, 0.0), axis=1, keepdims=True
    )

    def join(first, second):
        return jnp.where(low, first, second)

    def swap(value):
        return pltpu.roll(value, ROWS, 1)

    mask_copy.wait()

    @pl.loop(0, TILES)
    def _(step):
        tile = (me // 8 + (TILES - STRIDE) * step) % TILES
        group = recv.at[pl.ds(tile * 8, 8)]
        wait_on(group, p1_recv.at[tile])
        filled = []
        for q in range(4):
            columns = pl.ds(pl.multiple_of(tile * 512 + q * 128, 128), 128)
            first = recv[tile * 8 + 2 * q].astype(F32)
            second = recv[tile * 8 + 2 * q + 1].astype(F32)
            turned = (join(first, swap(second)), join(swap(first), second))
            keep = mask[:, columns] == 1
            pair = []
            for part in range(2):
                value = jnp.where(keep, data[part, :, columns].astype(F32), turned[part])
                weighted = (value * gains).astype(BF16)
                wb[tile, q // 2, part, :, q % 2 * 128:(q % 2 + 1) * 128] = weighted
                pair.append(value)
            filled.append(pair)
        for part in range(2):
            lanes = slice((1 - part) * 128, (2 - part) * 128)
            for half in range(2):
                first, second = filled[half][part], filled[2 + half][part]
                for odd, value in ((0, join(first, swap(second))), (1, join(swap(first), second))):
                    value = (-value).astype(BF16)
                    a_out[2 * half + odd, 0, tile, :, lanes] = value[:32]
                    a_out[2 * half + odd, 1, tile, :, lanes] = value[32:]

        d = (z - tile % 4 + 4) % 4
        for h in range(2):
            to_y = 2 * (d % 2) + h
            source = wb.at[tile, h]
            target = b0.at[d // 2, y, core, x // 2, :, x % 2]
            mine = jnp.logical_and(to_y == y, tile // 4 == x)

            @pl.when(mine)
            def _():
                pltpu.make_async_copy(source, target, b2_recv.at[d // 2]).start()

            @pl.when(jnp.logical_not(mine))
            def _():
                remote(source, target, b2_send, b2_recv.at[d // 2],
                       device(to_y, core, tile // 4, z)).start()
        for k in range(1, 4):
            to = (z + k) % 4
            for e in range(2):
                remote(a_out.at[to, e, tile], a0.at[e, tile, z], a2_send, a2_recv.at[e, z],
                       device(y, core, x, to)).start()

    for e in range(2):
        pltpu.make_async_copy(
            a_out.at[z, e], a0.at[e, pl.ds(0, TILES), z], a2_recv.at[e, z]
        ).start()

    def left_half(stage, e):
        return lefts[stage].at[e, pl.ds(0, TILES)]

    def right_half(stage, e):
        return rights[stage].at[e, :, core]

    def source_of(stage, e):
        return (0, e) if stage == 1 else (0, 1 - e) if stage == 2 else (1, e)

    def left_copy(stage, e):
        return remote(
            left_half(*source_of(stage, e)), left_half(stage, e),
            a3_send.at[stage - 1, e], a3_recv.at[stage - 1, e],
            device(y, core, (x + 1 + 2 * e) % 4, z),
        )

    def right_copy(stage, e):
        return remote(
            right_half(*source_of(stage, e)), right_half(stage, e),
            b3_send.at[stage - 1, e], b3_recv.at[stage - 1, e],
            device((y + 1 + 2 * e) % 4, core, x, z),
        )

    def sibling_copy(stage, e):
        return remote(
            right_half(stage, e), right_half(stage, e),
            s_send.at[stage, e], s_recv.at[stage, e], device(y, 1 - core, x, z),
        )

    def offset(stage, e):
        return 0 if stage == 0 else 2 if stage == 3 else 3 - 2 * e

    def half_of(stage, e):
        return 1 - e if stage == 2 else e

    def units(left_stage, right_stage):
        @pl.loop(0, 4)
        def _(step):
            ea, eb = step // 2, step % 2
            piece = (x + offset(left_stage, ea)) % 4
            half = half_of(left_stage, ea)
            yy = (y + offset(right_stage, eb)) % 4
            d = 2 * half_of(right_stage, eb) + yy // 2
            column = (z - d + 4) % 4
            used = lens_s[column, piece // 2, 0]
            total = None
            for slot in range(SLOTS):
                inner = lists[piece // 2, slot, x * 4 + column]
                left = lefts[left_stage][ea, jnp.where(slot < used, inner, TILES)].reshape(128, 256)
                right = rights[right_stage][eb, inner // 4, inner // 2 % 2, inner % 2].reshape(256, 256)
                upper = jnp.concatenate([left[:, 128:], -left[:, :128]], axis=1)
                wide = jnp.concatenate([upper, left], axis=0)
                term = jnp.dot(wide, right, preferred_element_type=F32)
                total = term if total is None else total + term
            h = yy % 2
            index = left_stage * 2 + ea
            held = c_out.at[index, d, h]
            total = total.reshape(2, 4, 32, 256)
            held[...] = total.astype(BF16)

            @pl.when(d == 0)
            def _():
                columns = pl.ds(pl.multiple_of(h * 256, 256), 256)
                mine[:, piece, :, half, :, columns] = total

            @pl.when(d == 1)
            def _():
                kept[index, 0, h] = total[:, :2]

            @pl.when(d == 3)
            def _():
                kept[index, 1, h] = total[:, 2:]

            @pl.when(d == 2)
            def _():
                for way in range(2):
                    remote(held.at[:, pl.ds(2 * way, 2)], relay.at[index, way, h],
                           c_send, r_recv.at[index, way, h],
                           device(y, core, x, (z + 3 - 2 * way) % 4)).start()

            @pl.when(d % 2 == 1)
            def _():
                rows = pl.ds(3 - d, 2)
                target = sum_place(d // 2, piece, half, h).at[:, rows]
                remote(held.at[:, rows], target, c_send, c_recv.at[d // 2],
                       device(y, core, x, column)).start()

    def sum_place(way, piece, half, h):
        columns = pl.ds(pl.multiple_of(h * 256, 256), 256)
        return c_in.at[way, :, piece, :, half, :, columns]

    def finish(first, last, h):
        @pl.loop(2 * first, 2 * last)
        def _(step):
            index, way = step // 2, step % 2
            stage, e = index // 2, index % 2
            near = jnp.logical_or(stage == 1, stage == 2)
            piece = (x + jnp.where(near, 3 - 2 * e, stage // 3 * 2)) % 4
            half = jnp.where(stage == 2, 1 - e, e)
            d = 2 * way + 1
            wait_on(relay.at[index, way, h], r_recv.at[index, way, h])
            rows = pl.ds(2 * way, 2)
            held = c_out.at[index, d, h, :, rows]
            held[...] = (kept[index, way, h] + relay[index, way, h].astype(F32)).astype(BF16)
            remote(held, sum_place(way, piece, half, h).at[:, rows], c_send, c_recv.at[way],
                   device(y, core, x, (z - d + 4) % 4)).start()

    for e in range(2):
        for part in range(4):
            wait_on(a0.at[e, pl.ds(0, TILES), part], a2_recv.at[e, part])
        left_copy(1, e).start()
    for e in range(2):
        wait_on(right_half(0, e), b2_recv.at[e])
        right_copy(1, e).start()
        sibling_copy(0, e).start()
    for e in range(2):
        right_copy(2, e).start()
        left_copy(2, e).start()

    for k in range(1, 4):
        length_copies[k - 1].wait_recv()
    pltpu.make_async_copy(lens_all, lens_s, l_copy.at[1]).start()
    pltpu.make_async_copy(lens_all, lens_s, l_copy.at[1]).wait()
    list_copy.wait()

    for e in range(2):
        sibling_copy(0, e).wait_recv()
    units(0, 0)
    soon, late = 1 - y % 2, y % 2
    for stage in range(1, 4):
        for e in range(2):
            wait_on(right_half(stage, e), b3_recv.at[stage - 1, e])
            sibling_copy(stage, e).start()
            if stage == 1:
                right_copy(3, e).start()
        for e in range(2):
            wait_on(left_half(stage, e), a3_recv.at[stage - 1, e])
            if stage == 1:
                left_copy(3, e).start()
        units(stage, 0)
        if stage == 2:
            units(2, 1)
        for e in range(2):
            sibling_copy(stage, e).wait_recv()
        for earlier in range(stage):
            units(earlier, stage)
        if stage < 3:
            units(stage, stage)
        if stage == 2:
            finish(0, 6, soon)
    units(3, 1)
    finish(0, 6, late)
    units(3, 2)
    units(3, 3)
    finish(6, 8, soon)
    finish(6, 8, late)

    wait_on(xt.at[pl.ds(0, DEVICES - 1)], p1_send)
    wait_on(wb.at[pl.ds(0, TILES - 1)], b2_send)
    wait_on(a_out.at[pl.ds(0, 3)], a2_send)
    for copy in length_copies:
        copy.wait_send()
    for e in range(2):
        for stage in range(4):
            sibling_copy(stage, e).wait_send()
        for stage in range(1, 4):
            left_copy(stage, e).wait_send()
            right_copy(stage, e).wait_send()
    wait_on(c_out.at[pl.ds(0, 6)], c_send)
    for way in range(2):
        wait_on(c_in.at[way], c_recv.at[way])


def local(data, fill_mask, obliquity, aperture, lengths):
    vmem = pl.BlockSpec(memory_space=pltpu.VMEM)
    far = pl.BlockSpec(memory_space=pl.ANY)
    dma = pltpu.SemaphoreType.DMA
    mine, sums = pl.pallas_call(
        kernel,
        out_shape=(
            pltpu.VMEM((2, 4, 4, 2, 32, TILE), F32), pltpu.VMEM((2, 2, 4, 4, 2, 32, TILE), BF16)
        ),
        in_specs=[far, far, vmem, vmem, far],
        out_specs=(vmem, vmem),
        scratch_shapes=[
            pltpu.VMEM(data.shape, BF16),
            pltpu.VMEM(fill_mask.shape, jnp.int32),
            pltpu.VMEM((DEVICES, ROWS, 128), BF16),
            pltpu.VMEM((DEVICES, ROWS, 128), BF16),
            pltpu.VMEM((TILES, 2, 2, ROWS, 256), BF16),
            pltpu.VMEM((4, 2, TILES, 32, 256), BF16),
        ]
        + [pltpu.VMEM((2, TILES + 1, 4, 32, 256), BF16)] * 4
        + [pltpu.VMEM((2, 4, 2, 2, 2, 2, ROWS, 256), BF16)] * 4
        + [
            pltpu.VMEM((8, 4, 2, 2, 4, 32, 256), BF16),
            pltpu.VMEM((8, 2, 2, 2, 2, 32, 256), BF16),
            pltpu.VMEM((8, 2, 2, 2, 2, 32, 256), F32),
            pltpu.VMEM((8, 128), jnp.int32),
            pltpu.VMEM((4, 8, 128), jnp.int32),
            pltpu.SMEM((4, 8, 128), jnp.int32),
            pltpu.SMEM((2, SLOTS, TILES), jnp.int32),
            dma(()), dma((16,)), dma((3,)), dma((3,)), dma((2,)), dma(()), dma((2, 4)), dma(()), dma((2,)),
            dma((3, 2)), dma((3, 2)), dma((3, 2)), dma((3, 2)), dma((4, 2)), dma((4, 2)), dma(()), dma((2,)),
            dma((8, 2, 2)),
            dma((2,)), pltpu.SemaphoreType.REGULAR,
        ],
        compiler_params=pltpu.CompilerParams(
            collective_id=1, has_side_effects=True, vmem_limit_bytes=54 * 1024 * 1024
        ),
        cost_estimate=pl.CostEstimate(
            flops=17_000_000_000, bytes_accessed=12_000_000, transcendentals=0
        ),
    )(data, fill_mask, obliquity.reshape(64, 128), lengths.T, jnp.swapaxes(aperture, 1, 2))
    total = mine + sums[0].astype(F32) + sums[1].astype(F32)
    return total.reshape(2, 2 * TILE, TILE)


def solution(mesh):
    placed = (
        P(None, ("src", "rcv"), None),
        P(("src", "rcv"), None),
        P(),
        P("src", None, None),
        P("src", "rcv"),
    )
    return jax.shard_map(
        local, mesh=mesh, in_specs=placed, out_specs=P(None, "src", "rcv"), check_vma=False
    )
```

```python
import jax
import jax.numpy as jnp
from jax import lax
from jax.experimental import pallas as pl
from jax.experimental.pallas import tpu as pltpu
from jax.sharding import PartitionSpec as P

TILE = 512
SLOTS = 8
TILES = 16
ROWS = 64
DEVICES = 128
STRIDE = 5
MESH = pl.DeviceIdType.MESH
F32 = jnp.float32
BF16 = jnp.bfloat16


def kernel(
    data_far, mask_far, gain, lens, aperture,
    mine, c_in,
    data, mask, xt, recv, wb, a_out, a0, a1, a2, a3, b0, b1, b2, b3, c_out, relay, kept, lens_own, lens_all, lens_s, lists,
    p1_send, p1_recv, l_send, l_recv, l_copy, a2_send, a2_recv, b2_send, b2_recv,
    a3_send, a3_recv, b3_send, b3_recv, s_send, s_recv, c_send, c_recv, r_recv, in_copy, met,
):
    src, rcv = lax.axis_index("src"), lax.axis_index("rcv")
    y, core = src // 2, src % 2
    x, z = rcv // 4, rcv % 4
    me = src * 16 + rcv
    lefts = (a0, a1, a2, a3)
    rights = (b0, b1, b2, b3)

    def device(yy, cc, xx, zz):
        return (yy * 2 + cc, xx * 4 + zz)

    def remote(source, target, send, got, to):
        return pltpu.make_async_remote_copy(
            src_ref=source, dst_ref=target, send_sem=send, recv_sem=got,
            device_id=to, device_id_type=MESH,
        )

    def wait_on(ref, sem):
        pltpu.make_async_copy(ref, ref, sem).wait()

    data_copy = pltpu.make_async_copy(data_far, data, in_copy.at[0])
    mask_copy = pltpu.make_async_copy(mask_far, mask, in_copy.at[1])
    list_copy = pltpu.make_async_copy(aperture, lists, l_copy.at[0])
    data_copy.start()
    mask_copy.start()
    list_copy.start()

    barrier = pltpu.get_barrier_semaphore()

    def tell(semaphore, others):
        for other in others:
            pl.semaphore_signal(semaphore, inc=1, device_id=other, device_id_type=MESH)

    def turn(first, last):
        @pl.loop(first, last)
        def _(step):
            for i in range(2):
                q = step * 2 + i
                block = data[:, :, pl.ds(pl.multiple_of(q * 256, 256), 256)].reshape(128, 256)
                xt[pl.ds(q * 4, 4)] = block.T.reshape(4, ROWS, 128)

    along_yz = [device((y + k // 4) % 4, core, x, (z + k) % 4) for k in range(1, 16)]
    across = [device(y, (core + k // 4) % 2, (x + k) % 4, z) for k in range(1, 8)]
    tell(barrier, along_yz + across)
    data_copy.wait()
    turn(0, 8)
    pl.semaphore_wait(barrier, 22)
    tell(met, across)
    turn(8, 16)
    pl.semaphore_wait(met, 7)

    def block_copy(target):
        return remote(xt.at[target], recv.at[me], p1_send, p1_recv.at[me // 8],
                      (target // 16, target % 16))

    pltpu.make_async_copy(xt.at[me], recv.at[me], p1_recv.at[me // 8]).start()
    for i in range(1, 8):
        block_copy(me // 8 * 8 + (me + i) % 8).start()

    @pl.loop(1, TILES)
    def _(step):
        tile = (me // 8 + STRIDE * step) % TILES
        for i in range(8):
            block_copy(tile * 8 + (me + i) % 8).start()

    lens_own[0:1, :] = jnp.broadcast_to(lens[:, 0:1], (1, 128))
    lens_own[1:2, :] = jnp.broadcast_to(lens[:, 1:2], (1, 128))
    lens_own[2:8, :] = jnp.zeros((6, 128), jnp.int32)
    lens_all[z] = lens_own[...]
    length_copies = []
    for k in range(1, 4):
        copy = remote(lens_own, lens_all.at[z], l_send.at[k - 1], l_recv.at[k - 1],
                      device(y, core, x, (z + k) % 4))
        copy.start()
        length_copies.append(copy)

    for buf in lefts:
        for e in range(2):
            buf[e, TILES] = jnp.zeros((4, 32, 256), BF16)

    lane = lax.broadcasted_iota(jnp.int32, (ROWS, 128), 1)
    low = lane < ROWS
    row = lax.broadcasted_iota(jnp.int32, (ROWS, 128), 0)
    gain_row = jnp.broadcast_to(gain[pl.ds(me // 2, 1), :], (ROWS, 128))
    gains = jnp.sum(
        jnp.where(lane == row + (me % 2) * ROWS, gain_row, 0.0), axis=1, keepdims=True
    )

    def join(first, second):
        return jnp.where(low, first, second)

    def swap(value):
        return pltpu.roll(value, ROWS, 1)

    mask_copy.wait()

    @pl.loop(0, TILES)
    def _(step):
        tile = (me // 8 + (TILES - STRIDE) * step) % TILES
        group = recv.at[pl.ds(tile * 8, 8)]
        wait_on(group, p1_recv.at[tile])
        filled = []
        for q in range(4):
            columns = pl.ds(pl.multiple_of(tile * 512 + q * 128, 128), 128)
            first = recv[tile * 8 + 2 * q].astype(F32)
            second = recv[tile * 8 + 2 * q + 1].astype(F32)
            turned = (join(first, swap(second)), join(swap(first), second))
            keep = mask[:, columns] == 1
            pair = []
            for part in range(2):
                value = jnp.where(keep, data[part, :, columns].astype(F32), turned[part])
                weighted = (value * gains).astype(BF16)
                wb[tile, q // 2, part, :, q % 2 * 128:(q % 2 + 1) * 128] = weighted
                pair.append(value)
            filled.append(pair)
        for part in range(2):
            lanes = slice((1 - part) * 128, (2 - part) * 128)
            for half in range(2):
                first, second = filled[half][part], filled[2 + half][part]
                for odd, value in ((0, join(first, swap(second))), (1, join(swap(first), second))):
                    value = (-value).astype(BF16)
                    a_out[2 * half + odd, 0, tile, :, lanes] = value[:32]
                    a_out[2 * half + odd, 1, tile, :, lanes] = value[32:]

        d = (z - tile % 4 + 4) % 4
        for h in range(2):
            to_y = 2 * (d % 2) + h
            source = wb.at[tile, h]
            target = b0.at[d // 2, y, core, x // 2, :, x % 2]
            mine = jnp.logical_and(to_y == y, tile // 4 == x)

            @pl.when(mine)
            def _():
                pltpu.make_async_copy(source, target, b2_recv.at[d // 2, y]).start()

            @pl.when(jnp.logical_not(mine))
            def _():
                remote(source, target, b2_send, b2_recv.at[d // 2, y],
                       device(to_y, core, tile // 4, z)).start()
        for k in range(1, 4):
            to = (z + k) % 4
            for e in range(2):
                remote(a_out.at[to, e, tile], a0.at[e, tile, z], a2_send, a2_recv.at[e, z],
                       device(y, core, x, to)).start()

    for e in range(2):
        pltpu.make_async_copy(
            a_out.at[z, e], a0.at[e, pl.ds(0, TILES), z], a2_recv.at[e, z]
        ).start()

    def left_half(stage, e):
        return lefts[stage].at[e, pl.ds(0, TILES)]

    def right_half(stage, e):
        return rights[stage].at[e, :, core]

    def source_of(stage, e):
        return (0, e) if stage == 1 else (0, 1 - e) if stage == 2 else (1, e)

    def left_copy(stage, e):
        return remote(
            left_half(*source_of(stage, e)), left_half(stage, e),
            a3_send.at[stage - 1, e], a3_recv.at[stage - 1, e],
            device(y, core, (x + 1 + 2 * e) % 4, z),
        )

    def right_copy(stage, e):
        return remote(
            right_half(*source_of(stage, e)), right_half(stage, e),
            b3_send.at[stage - 1, e], b3_recv.at[stage - 1, e],
            device((y + 1 + 2 * e) % 4, core, x, z),
        )

    def sibling_copy(stage, e):
        return remote(
            right_half(stage, e), right_half(stage, e),
            s_send.at[stage, e], s_recv.at[stage, e], device(y, 1 - core, x, z),
        )

    def offset(stage, e):
        return 0 if stage == 0 else 2 if stage == 3 else 3 - 2 * e

    def half_of(stage, e):
        return 1 - e if stage == 2 else e

    def units(left_stage, right_stage):
        @pl.loop(0, 4)
        def _(step):
            ea, eb = step // 2, step % 2
            piece = (x + offset(left_stage, ea)) % 4
            half = half_of(left_stage, ea)
            yy = (y + offset(right_stage, eb)) % 4
            d = 2 * half_of(right_stage, eb) + yy // 2
            column = (z - d + 4) % 4
            used = lens_s[column, piece // 2, 0]
            total = None
            for slot in range(SLOTS):
                inner = lists[piece // 2, slot, x * 4 + column]
                left = lefts[left_stage][ea, jnp.where(slot < used, inner, TILES)].reshape(128, 256)
                right = rights[right_stage][eb, inner // 4, inner // 2 % 2, inner % 2].reshape(256, 256)
                upper = jnp.concatenate([left[:, 128:], -left[:, :128]], axis=1)
                wide = jnp.concatenate([upper, left], axis=0)
                term = jnp.dot(wide, right, preferred_element_type=F32)
                total = term if total is None else total + term
            h = yy % 2
            index = left_stage * 2 + ea
            held = c_out.at[index, d, h]
            total = total.reshape(2, 4, 32, 256)
            held[...] = total.astype(BF16)

            @pl.when(d == 0)
            def _():
                columns = pl.ds(pl.multiple_of(h * 256, 256), 256)
                mine[:, piece, :, half, :, columns] = total

            @pl.when(d == 1)
            def _():
                kept[index, 0, h] = total[:, :2]

            @pl.when(d == 3)
            def _():
                kept[index, 1, h] = total[:, 2:]

            @pl.when(d == 2)
            def _():
                for way in range(2):
                    remote(held.at[:, pl.ds(2 * way, 2)], relay.at[index, way, h],
                           c_send, r_recv.at[index, way, h],
                           device(y, core, x, (z + 3 - 2 * way) % 4)).start()

            @pl.when(d % 2 == 1)
            def _():
                rows = pl.ds(3 - d, 2)
                target = sum_place(d // 2, piece, half, h).at[:, rows]
                remote(held.at[:, rows], target, c_send, c_recv.at[d // 2],
                       device(y, core, x, column)).start()

    def sum_place(way, piece, half, h):
        columns = pl.ds(pl.multiple_of(h * 256, 256), 256)
        return c_in.at[way, :, piece, :, half, :, columns]

    def finish(first, last, h):
        @pl.loop(2 * first, 2 * last)
        def _(step):
            index, way = step // 2, step % 2
            stage, e = index // 2, index % 2
            near = jnp.logical_or(stage == 1, stage == 2)
            piece = (x + jnp.where(near, 3 - 2 * e, stage // 3 * 2)) % 4
            half = jnp.where(stage == 2, 1 - e, e)
            d = 2 * way + 1
            wait_on(relay.at[index, way, h], r_recv.at[index, way, h])
            rows = pl.ds(2 * way, 2)
            held = c_out.at[index, d, h, :, rows]
            held[...] = (kept[index, way, h] + relay[index, way, h].astype(F32)).astype(BF16)
            remote(held, sum_place(way, piece, half, h).at[:, rows], c_send, c_recv.at[way],
                   device(y, core, x, (z - d + 4) % 4)).start()

    for i in range(4):
        for e in range(2):
            part = (z + i) % 4
            source = a0.at[e, pl.ds(0, TILES), part]
            wait_on(source, a2_recv.at[e, part])
            remote(source, a1.at[e, pl.ds(0, TILES), part], a3_send.at[0, e], a3_recv.at[0, e],
                   device(y, core, (x + 1 + 2 * e) % 4, z)).start()
        for e in range(2):
            part = (y + i) % 4
            source = b0.at[e, part, core]
            wait_on(source, b2_recv.at[e, part])
            remote(source, b1.at[e, part, core], b3_send.at[0, e], b3_recv.at[0, e],
                   device((y + 1 + 2 * e) % 4, core, x, z)).start()
    for e in range(2):
        sibling_copy(0, e).start()
    for e in range(2):
        right_copy(2, e).start()
        left_copy(2, e).start()

    for k in range(1, 4):
        length_copies[k - 1].wait_recv()
    pltpu.make_async_copy(lens_all, lens_s, l_copy.at[1]).start()
    pltpu.make_async_copy(lens_all, lens_s, l_copy.at[1]).wait()
    list_copy.wait()

    for e in range(2):
        sibling_copy(0, e).wait_recv()
    units(0, 0)
    soon, late = 1 - y % 2, y % 2
    for stage in range(1, 4):
        for e in range(2):
            wait_on(right_half(stage, e), b3_recv.at[stage - 1, e])
            sibling_copy(stage, e).start()
            if stage == 1:
                right_copy(3, e).start()
        for e in range(2):
            wait_on(left_half(stage, e), a3_recv.at[stage - 1, e])
            if stage == 1:
                left_copy(3, e).start()
        units(stage, 0)
        if stage == 2:
            units(2, 1)
        for e in range(2):
            sibling_copy(stage, e).wait_recv()
        for earlier in range(stage):
            units(earlier, stage)
        if stage < 3:
            units(stage, stage)
        if stage == 2:
            finish(0, 6, soon)
    units(3, 1)
    finish(0, 6, late)
    units(3, 2)
    units(3, 3)
    finish(6, 8, soon)
    finish(6, 8, late)

    wait_on(xt.at[pl.ds(0, DEVICES - 1)], p1_send)
    wait_on(wb.at[pl.ds(0, TILES - 1)], b2_send)
    wait_on(a_out.at[pl.ds(0, 3)], a2_send)
    for copy in length_copies:
        copy.wait_send()
    for e in range(2):
        for stage in range(4):
            sibling_copy(stage, e).wait_send()
        for stage in range(1, 4):
            left_copy(stage, e).wait_send()
            right_copy(stage, e).wait_send()
    wait_on(c_out.at[pl.ds(0, 6)], c_send)
    for way in range(2):
        wait_on(c_in.at[way], c_recv.at[way])


def local(data, fill_mask, obliquity, aperture, lengths):
    vmem = pl.BlockSpec(memory_space=pltpu.VMEM)
    far = pl.BlockSpec(memory_space=pl.ANY)
    dma = pltpu.SemaphoreType.DMA
    mine, sums = pl.pallas_call(
        kernel,
        out_shape=(
            pltpu.VMEM((2, 4, 4, 2, 32, TILE), F32), pltpu.VMEM((2, 2, 4, 4, 2, 32, TILE), BF16)
        ),
        in_specs=[far, far, vmem, vmem, far],
        out_specs=(vmem, vmem),
        scratch_shapes=[
            pltpu.VMEM(data.shape, BF16),
            pltpu.VMEM(fill_mask.shape, jnp.int32),
            pltpu.VMEM((DEVICES, ROWS, 128), BF16),
            pltpu.VMEM((DEVICES, ROWS, 128), BF16),
            pltpu.VMEM((TILES, 2, 2, ROWS, 256), BF16),
            pltpu.VMEM((4, 2, TILES, 32, 256), BF16),
        ]
        + [pltpu.VMEM((2, TILES + 1, 4, 32, 256), BF16)] * 4
        + [pltpu.VMEM((2, 4, 2, 2, 2, 2, ROWS, 256), BF16)] * 4
        + [
            pltpu.VMEM((8, 4, 2, 2, 4, 32, 256), BF16),
            pltpu.VMEM((8, 2, 2, 2, 2, 32, 256), BF16),
            pltpu.VMEM((8, 2, 2, 2, 2, 32, 256), F32),
            pltpu.VMEM((8, 128), jnp.int32),
            pltpu.VMEM((4, 8, 128), jnp.int32),
            pltpu.SMEM((4, 8, 128), jnp.int32),
            pltpu.SMEM((2, SLOTS, TILES), jnp.int32),
            dma(()), dma((16,)), dma((3,)), dma((3,)), dma((2,)), dma(()), dma((2, 4)), dma(()), dma((2, 4)),
            dma((3, 2)), dma((3, 2)), dma((3, 2)), dma((3, 2)), dma((4, 2)), dma((4, 2)), dma(()), dma((2,)),
            dma((8, 2, 2)),
            dma((2,)), pltpu.SemaphoreType.REGULAR,
        ],
        compiler_params=pltpu.CompilerParams(
            collective_id=1, has_side_effects=True, vmem_limit_bytes=54 * 1024 * 1024
        ),
        cost_estimate=pl.CostEstimate(
            flops=17_000_000_000, bytes_accessed=12_000_000, transcendentals=0
        ),
    )(data, fill_mask, obliquity.reshape(64, 128), lengths.T, jnp.swapaxes(aperture, 1, 2))
    total = mine + sums[0].astype(F32) + sums[1].astype(F32)
    return total.reshape(2, 2 * TILE, TILE)


def solution(mesh):
    placed = (
        P(None, ("src", "rcv"), None),
        P(("src", "rcv"), None),
        P(),
        P("src", None, None),
        P("src", "rcv"),
    )
    return jax.shard_map(
        local, mesh=mesh, in_specs=placed, out_specs=P(None, "src", "rcv"), check_vma=False
    )
```

```python
import jax
import jax.numpy as jnp
from jax import lax
from jax.experimental import pallas as pl
from jax.experimental.pallas import tpu as pltpu
from jax.sharding import PartitionSpec as P

TILE = 512
SLOTS = 8
TILES = 16
ROWS = 64
DEVICES = 128
STRIDE = 5
MESH = pl.DeviceIdType.MESH
F32 = jnp.float32
BF16 = jnp.bfloat16


def kernel(
    data_far, mask_far, gain, lens, aperture,
    mine, c_in,
    data, mask, xt, recv, wb, a_out, a0, a1, a2, a3, b0, b1, b2, b3, c_out, relay, kept, lens_own, lens_all, lens_s, lists,
    p1_send, p1_recv, l_send, l_recv, l_copy, a2_send, a2_recv, b2_send, b2_recv,
    a3_send, a3_recv, b3_send, b3_recv, s_send, s_recv, c_send, c_recv, r_recv, in_copy, met,
):
    src, rcv = lax.axis_index("src"), lax.axis_index("rcv")
    y, core = src // 2, src % 2
    x, z = rcv // 4, rcv % 4
    me = src * 16 + rcv
    lefts = (a0, a1, a2, a3)
    rights = (b0, b1, b2, b3)

    def device(yy, cc, xx, zz):
        return (yy * 2 + cc, xx * 4 + zz)

    def remote(source, target, send, got, to):
        return pltpu.make_async_remote_copy(
            src_ref=source, dst_ref=target, send_sem=send, recv_sem=got,
            device_id=to, device_id_type=MESH,
        )

    def wait_on(ref, sem):
        pltpu.make_async_copy(ref, ref, sem).wait()

    data_copy = pltpu.make_async_copy(data_far, data, in_copy.at[0])
    mask_copy = pltpu.make_async_copy(mask_far, mask, in_copy.at[1])
    list_copy = pltpu.make_async_copy(aperture, lists, l_copy.at[0])
    data_copy.start()
    mask_copy.start()
    list_copy.start()

    barrier = pltpu.get_barrier_semaphore()

    def tell(semaphore, others):
        for other in others:
            pl.semaphore_signal(semaphore, inc=1, device_id=other, device_id_type=MESH)

    def turn(first, last):
        @pl.loop(first, last)
        def _(step):
            for i in range(2):
                q = step * 2 + i
                block = data[:, :, pl.ds(pl.multiple_of(q * 256, 256), 256)].reshape(128, 256)
                xt[pl.ds(q * 4, 4)] = block.T.reshape(4, ROWS, 128)

    along_yz = [device((y + k // 4) % 4, core, x, (z + k) % 4) for k in range(1, 16)]
    across = [device(y, (core + k // 4) % 2, (x + k) % 4, z) for k in range(1, 8)]
    tell(barrier, along_yz + across)
    data_copy.wait()
    turn(0, 8)
    pl.semaphore_wait(barrier, 22)
    tell(met, across)
    turn(8, 16)
    pl.semaphore_wait(met, 7)

    def block_copy(target):
        return remote(xt.at[target], recv.at[me], p1_send, p1_recv.at[me // 8],
                      (target // 16, target % 16))

    pltpu.make_async_copy(xt.at[me], recv.at[me], p1_recv.at[me // 8]).start()
    for i in range(1, 8):
        block_copy(me // 8 * 8 + (me + i) % 8).start()

    @pl.loop(1, TILES)
    def _(step):
        tile = (me // 8 + STRIDE * step) % TILES
        for i in range(8):
            block_copy(tile * 8 + (me + i) % 8).start()

    lens_own[0:1, :] = jnp.broadcast_to(lens[:, 0:1], (1, 128))
    lens_own[1:2, :] = jnp.broadcast_to(lens[:, 1:2], (1, 128))
    lens_own[2:8, :] = jnp.zeros((6, 128), jnp.int32)
    lens_all[z] = lens_own[...]
    length_copies = []
    for k in range(1, 4):
        copy = remote(lens_own, lens_all.at[z], l_send.at[k - 1], l_recv.at[k - 1],
                      device(y, core, x, (z + k) % 4))
        copy.start()
        length_copies.append(copy)

    for buf in lefts:
        for e in range(2):
            buf[e, TILES] = jnp.zeros((4, 32, 256), BF16)

    lane = lax.broadcasted_iota(jnp.int32, (ROWS, 128), 1)
    low = lane < ROWS
    row = lax.broadcasted_iota(jnp.int32, (ROWS, 128), 0)
    gain_row = jnp.broadcast_to(gain[pl.ds(me // 2, 1), :], (ROWS, 128))
    gains = jnp.sum(
        jnp.where(lane == row + (me % 2) * ROWS, gain_row, 0.0), axis=1, keepdims=True
    )

    def join(first, second):
        return jnp.where(low, first, second)

    def swap(value):
        return pltpu.roll(value, ROWS, 1)

    mask_copy.wait()

    @pl.loop(0, TILES)
    def _(step):
        tile = (me // 8 + (TILES - STRIDE) * step) % TILES
        group = recv.at[pl.ds(tile * 8, 8)]
        wait_on(group, p1_recv.at[tile])
        filled = []
        for q in range(4):
            columns = pl.ds(pl.multiple_of(tile * 512 + q * 128, 128), 128)
            first = recv[tile * 8 + 2 * q].astype(F32)
            second = recv[tile * 8 + 2 * q + 1].astype(F32)
            turned = (join(first, swap(second)), join(swap(first), second))
            keep = mask[:, columns] == 1
            pair = []
            for part in range(2):
                value = jnp.where(keep, data[part, :, columns].astype(F32), turned[part])
                weighted = (value * gains).astype(BF16)
                wb[tile, q // 2, part, :, q % 2 * 128:(q % 2 + 1) * 128] = weighted
                pair.append(value)
            filled.append(pair)
        for part in range(2):
            lanes = slice((1 - part) * 128, (2 - part) * 128)
            for half in range(2):
                first, second = filled[half][part], filled[2 + half][part]
                for odd, value in ((0, join(first, swap(second))), (1, join(swap(first), second))):
                    value = (-value).astype(BF16)
                    a_out[2 * half + odd, 0, tile, :, lanes] = value[:32]
                    a_out[2 * half + odd, 1, tile, :, lanes] = value[32:]

        d = (z - tile % 4 + 4) % 4
        for h in range(2):
            to_y = 2 * (d % 2) + h
            source = wb.at[tile, h]
            target = b0.at[d // 2, y, core, x // 2, :, x % 2]
            mine = jnp.logical_and(to_y == y, tile // 4 == x)

            @pl.when(mine)
            def _():
                pltpu.make_async_copy(source, target, b2_recv.at[d // 2, y]).start()

            @pl.when(jnp.logical_not(mine))
            def _():
                remote(source, target, b2_send, b2_recv.at[d // 2, y],
                       device(to_y, core, tile // 4, z)).start()
        for k in range(1, 4):
            to = (z + k) % 4
            for e in range(2):
                remote(a_out.at[to, e, tile], a0.at[e, tile, z], a2_send, a2_recv.at[e, z],
                       device(y, core, x, to)).start()

    for e in range(2):
        pltpu.make_async_copy(
            a_out.at[z, e], a0.at[e, pl.ds(0, TILES), z], a2_recv.at[e, z]
        ).start()

    def left_half(stage, e):
        return lefts[stage].at[e, pl.ds(0, TILES)]

    def right_half(stage, e):
        return rights[stage].at[e, :, core]

    def source_of(stage, e):
        return (0, e) if stage == 1 else (0, 1 - e) if stage == 2 else (1, e)

    def left_copy(stage, e):
        return remote(
            left_half(*source_of(stage, e)), left_half(stage, e),
            a3_send.at[stage - 1, e], a3_recv.at[stage - 1, e],
            device(y, core, (x + 1 + 2 * e) % 4, z),
        )

    def right_copy(stage, e):
        return remote(
            right_half(*source_of(stage, e)), right_half(stage, e),
            b3_send.at[stage - 1, e], b3_recv.at[stage - 1, e],
            device((y + 1 + 2 * e) % 4, core, x, z),
        )

    def sibling_copy(stage, e):
        return remote(
            right_half(stage, e), right_half(stage, e),
            s_send.at[stage, e], s_recv.at[stage, e], device(y, 1 - core, x, z),
        )

    def offset(stage, e):
        return 0 if stage == 0 else 2 if stage == 3 else 3 - 2 * e

    def half_of(stage, e):
        return 1 - e if stage == 2 else e

    def units(left_stage, right_stage):
        @pl.loop(0, 4)
        def _(step):
            ea, eb = step // 2, step % 2
            piece = (x + offset(left_stage, ea)) % 4
            half = half_of(left_stage, ea)
            yy = (y + offset(right_stage, eb)) % 4
            d = 2 * half_of(right_stage, eb) + yy // 2
            column = (z - d + 4) % 4
            used = lens_s[column, piece // 2, 0]
            total = None
            for slot in range(SLOTS):
                inner = lists[piece // 2, slot, x * 4 + column]
                left = lefts[left_stage][ea, jnp.where(slot < used, inner, TILES)].reshape(128, 256)
                right = rights[right_stage][eb, inner // 4, inner // 2 % 2, inner % 2].reshape(256, 256)
                upper = jnp.concatenate([left[:, 128:], -left[:, :128]], axis=1)
                wide = jnp.concatenate([upper, left], axis=0)
                term = jnp.dot(wide, right, preferred_element_type=F32)
                total = term if total is None else total + term
            h = yy % 2
            index = left_stage * 2 + ea
            held = c_out.at[index, d, h]
            total = total.reshape(2, 4, 32, 256)
            held[...] = total.astype(BF16)

            @pl.when(d == 0)
            def _():
                columns = pl.ds(pl.multiple_of(h * 256, 256), 256)
                mine[:, piece, :, half, :, columns] = total

            @pl.when(d == 1)
            def _():
                kept[index, 0, h] = total[:, :2]

            @pl.when(d == 3)
            def _():
                kept[index, 1, h] = total[:, 2:]

            @pl.when(d == 2)
            def _():
                for way in range(2):
                    remote(held.at[:, pl.ds(2 * way, 2)], relay.at[index, way, h],
                           c_send, r_recv.at[index, way, h],
                           device(y, core, x, (z + 3 - 2 * way) % 4)).start()

            @pl.when(d % 2 == 1)
            def _():
                rows = pl.ds(3 - d, 2)
                target = sum_place(d // 2, piece, half, h).at[:, rows]
                remote(held.at[:, rows], target, c_send, c_recv.at[d // 2],
                       device(y, core, x, column)).start()

    def sum_place(way, piece, half, h):
        columns = pl.ds(pl.multiple_of(h * 256, 256), 256)
        return c_in.at[way, :, piece, :, half, :, columns]

    def finish(first, last, h):
        @pl.loop(2 * first, 2 * last)
        def _(step):
            index, way = step // 2, step % 2
            stage, e = index // 2, index % 2
            near = jnp.logical_or(stage == 1, stage == 2)
            piece = (x + jnp.where(near, 3 - 2 * e, stage // 3 * 2)) % 4
            half = jnp.where(stage == 2, 1 - e, e)
            d = 2 * way + 1
            wait_on(relay.at[index, way, h], r_recv.at[index, way, h])
            rows = pl.ds(2 * way, 2)
            held = c_out.at[index, d, h, :, rows]
            held[...] = (kept[index, way, h] + relay[index, way, h].astype(F32)).astype(BF16)
            remote(held, sum_place(way, piece, half, h).at[:, rows], c_send, c_recv.at[way],
                   device(y, core, x, (z - d + 4) % 4)).start()

    for i in range(4):
        for e in range(2):
            part = (z + i) % 4
            source = a0.at[e, pl.ds(0, TILES), part]
            wait_on(source, a2_recv.at[e, part])
            remote(source, a1.at[e, pl.ds(0, TILES), part], a3_send.at[0, e], a3_recv.at[0, e],
                   device(y, core, (x + 1 + 2 * e) % 4, z)).start()
        for e in range(2):
            part = (y + i) % 4
            source = b0.at[e, part, core]
            wait_on(source, b2_recv.at[e, part])
            remote(source, b1.at[e, part, core], b3_send.at[0, e], b3_recv.at[0, e],
                   device((y + 1 + 2 * e) % 4, core, x, z)).start()
    for e in range(2):
        sibling_copy(0, e).start()
    for e in range(2):
        right_copy(2, e).start()
        left_copy(2, e).start()

    for k in range(1, 4):
        length_copies[k - 1].wait_recv()
    pltpu.make_async_copy(lens_all, lens_s, l_copy.at[1]).start()
    pltpu.make_async_copy(lens_all, lens_s, l_copy.at[1]).wait()
    list_copy.wait()

    for e in range(2):
        sibling_copy(0, e).wait_recv()
    units(0, 0)
    soon, late = 1 - y % 2, y % 2
    for stage in range(1, 4):
        for e in range(2):
            wait_on(right_half(stage, e), b3_recv.at[stage - 1, e])
            sibling_copy(stage, e).start()
            if stage == 1:
                right_copy(3, e).start()
        for e in range(2):
            wait_on(left_half(stage, e), a3_recv.at[stage - 1, e])
            if stage == 1:
                left_copy(3, e).start()
        units(stage, 0)
        if stage == 2:
            units(2, 1)
        for e in range(2):
            sibling_copy(stage, e).wait_recv()
        for earlier in range(stage):
            units(earlier, stage)
        if stage < 3:
            units(stage, stage)
        if stage == 2:
            finish(0, 6, soon)
    units(3, 3)
    finish(0, 6, late)
    units(3, 1)
    units(3, 2)
    finish(6, 8, late)
    finish(6, 8, soon)

    wait_on(xt.at[pl.ds(0, DEVICES - 1)], p1_send)
    wait_on(wb.at[pl.ds(0, TILES - 1)], b2_send)
    wait_on(a_out.at[pl.ds(0, 3)], a2_send)
    for copy in length_copies:
        copy.wait_send()
    for e in range(2):
        for stage in range(4):
            sibling_copy(stage, e).wait_send()
        for stage in range(1, 4):
            left_copy(stage, e).wait_send()
            right_copy(stage, e).wait_send()
    wait_on(c_out.at[pl.ds(0, 6)], c_send)
    for way in range(2):
        wait_on(c_in.at[way], c_recv.at[way])


def local(data, fill_mask, obliquity, aperture, lengths):
    vmem = pl.BlockSpec(memory_space=pltpu.VMEM)
    far = pl.BlockSpec(memory_space=pl.ANY)
    dma = pltpu.SemaphoreType.DMA
    mine, sums = pl.pallas_call(
        kernel,
        out_shape=(
            pltpu.VMEM((2, 4, 4, 2, 32, TILE), F32), pltpu.VMEM((2, 2, 4, 4, 2, 32, TILE), BF16)
        ),
        in_specs=[far, far, vmem, vmem, far],
        out_specs=(vmem, vmem),
        scratch_shapes=[
            pltpu.VMEM(data.shape, BF16),
            pltpu.VMEM(fill_mask.shape, jnp.int32),
            pltpu.VMEM((DEVICES, ROWS, 128), BF16),
            pltpu.VMEM((DEVICES, ROWS, 128), BF16),
            pltpu.VMEM((TILES, 2, 2, ROWS, 256), BF16),
            pltpu.VMEM((4, 2, TILES, 32, 256), BF16),
        ]
        + [pltpu.VMEM((2, TILES + 1, 4, 32, 256), BF16)] * 4
        + [pltpu.VMEM((2, 4, 2, 2, 2, 2, ROWS, 256), BF16)] * 4
        + [
            pltpu.VMEM((8, 4, 2, 2, 4, 32, 256), BF16),
            pltpu.VMEM((8, 2, 2, 2, 2, 32, 256), BF16),
            pltpu.VMEM((8, 2, 2, 2, 2, 32, 256), F32),
            pltpu.VMEM((8, 128), jnp.int32),
            pltpu.VMEM((4, 8, 128), jnp.int32),
            pltpu.SMEM((4, 8, 128), jnp.int32),
            pltpu.SMEM((2, SLOTS, TILES), jnp.int32),
            dma(()), dma((16,)), dma((3,)), dma((3,)), dma((2,)), dma(()), dma((2, 4)), dma(()), dma((2, 4)),
            dma((3, 2)), dma((3, 2)), dma((3, 2)), dma((3, 2)), dma((4, 2)), dma((4, 2)), dma(()), dma((2,)),
            dma((8, 2, 2)),
            dma((2,)), pltpu.SemaphoreType.REGULAR,
        ],
        compiler_params=pltpu.CompilerParams(
            collective_id=1, has_side_effects=True, vmem_limit_bytes=54 * 1024 * 1024
        ),
        cost_estimate=pl.CostEstimate(
            flops=17_000_000_000, bytes_accessed=12_000_000, transcendentals=0
        ),
    )(data, fill_mask, obliquity.reshape(64, 128), lengths.T, jnp.swapaxes(aperture, 1, 2))
    total = mine + sums[0].astype(F32) + sums[1].astype(F32)
    return total.reshape(2, 2 * TILE, TILE)


def solution(mesh):
    placed = (
        P(None, ("src", "rcv"), None),
        P(("src", "rcv"), None),
        P(),
        P("src", None, None),
        P("src", "rcv"),
    )
    return jax.shard_map(
        local, mesh=mesh, in_specs=placed, out_specs=P(None, "src", "rcv"), check_vma=False
    )
```
